128 devices in a mesh: stream: 32 (over x, z, core), span: 4 (over y).
Axes of the slice: x: 4, y: 4, z: 4, core: 2. Of those that a mesh axis runs over, the one named last changes fastest.
Arguments:
- basis: float32 [4, 64, 65536], P(None, None, ('stream', 'span')), may hold values from -5.6 to 5.6
- interface_row_owner: int32 [131072, 1], P(('stream', 'span')), may hold values from 0 to 127; in each aligned block of 1024 rows (0 to 1023, 1024 to 2047, ...) at most 16 rows name the same one
- interface_local_row: int32 [131072], P(('stream', 'span')), may hold values from 0 to 511
- interface_slot_weight: float32 [131072], P(('stream', 'span')), may hold values from 0.25 to 1
- local_inverse: bfloat16 [64, 64, 131072], P(None, None, ('stream', 'span')), may hold values from -0.75 to 1.55
- prim_index: int32 [4096], P(('stream', 'span')), may hold values from 0 to 1023
- prim_vector: float32 [64, 4096], P(None, ('stream', 'span')), may hold values from -4 to 4
- coarse_inverse: float32 [1024, 1024], P('stream'), may hold values from -0.1875 to 0.1875
- interface_shifted_diagonal: float32 [64, 131072], P(None, ('stream', 'span')), may hold values from 2 to 4
- coupling_index: int32 [2, 65536], P(None, ('stream', 'span')), may hold values from 0 to 1023
- coupling_blocks: bfloat16 [2, 64, 64, 65536], P(None, None, None, ('stream', 'span')), may hold values from -0.75 to 0.75
- interior_inverse: bfloat16 [64, 64, 65536], P(None, None, ('stream', 'span')), may hold values from -0.75 to 1.55
Outputs:
- direction: float32 [64, 65536], P(None, ('stream', 'span'))
- coeffs: float32 [5], replicated
The draws below stay inside these ranges and needn't reach their ends.
Inputs may be any that keep to these rules, and one draw needn't show every extreme that they name: `interface_row_owner`: in the slots of one subdomain (aligned blocks of 1024 slots) no owner is named more than 16 times, a bound that some block reaches.
All inputs are finite; a program needn't handle non-finite values.
Results may differ from the reference program's by a relative error of at most 0.0003.
Values sent between devices are 32-bit elements; how exact they have to be, the bound alone decides.
No kernel may reach another device: no remote copies, remote signals or barrier semaphores. Data moves between devices by JAX's collectives and lax.ppermute only.
A program may use at most 64 MiB of HBM per device.

```python
import math
import jax
import jax.numpy as jnp
import numpy as np
from jax import lax

BLOCK_REALS = 64
BOUNDARY_SLOTS = 1024
NIN = 512
KC = 2
NPRIM = 32
KB = 4
ROWS_PER_OWNER = 512
SUBDOMAIN_SLOTS = 16
NG = 65536
TOTAL_SLOTS = 131072
NINT = 65536
NCS = 1024
N_STREAM = 32
N_SPAN = 4
DEVICES = 128


def sample_block(key, count):
    ident = (jnp.arange(BLOCK_REALS)[:, None] == jnp.arange(BLOCK_REALS)[None, :]).astype(jnp.float32)
    noise = jnp.clip(jax.random.normal(key, (BLOCK_REALS, BLOCK_REALS, count), jnp.float32) / 8.0, -0.75, 0.75)
    values = noise + 0.6 * ident[:, :, None]
    return values.astype(jnp.bfloat16)


def draw_local_inverse(key, part):
    return sample_block(jax.random.fold_in(key, 101), TOTAL_SLOTS)


def draw_interior_inverse(key, part):
    return sample_block(jax.random.fold_in(key, 202), NINT)


def draw_basis(key, part):
    base = jax.random.fold_in(key, 303)
    first = jax.random.fold_in(base, 1)
    second = jax.random.fold_in(base, 2)
    common = jnp.clip(jax.random.normal(first, (BLOCK_REALS, NG), jnp.float32), -4.0, 4.0)
    owned_rows = jnp.clip(jax.random.normal(second, (KB, BLOCK_REALS, NG), jnp.float32), -4.0, 4.0)
    values = 0.6 * common[None] + 0.8 * owned_rows
    return values.astype(jnp.float32)


def touch_ends(values, key, low, largest):
    extent = values.shape
    spot = [jax.random.randint(jax.random.fold_in(key, axis), (), 0, extent[axis]) for axis in range(len(extent))]
    values = values.at[tuple(spot)].set(low)
    longest = extent.index(max(extent))
    spot[longest] = (spot[longest] + 1) % extent[longest]
    return values.at[tuple(spot)].set(largest)


def steps_of(rng, extent, pieces, least, largest):
    gain, own = 1.0, jax.random.fold_in(rng, 6)
    for dim, shards_of in pieces:
        heights = jnp.exp(jax.random.uniform(jax.random.fold_in(own, dim), (shards_of,), jnp.float32, least / len(pieces), largest / len(pieces)))
        gain = gain * jnp.repeat(heights, extent[dim] // shards_of).reshape([-1 if axis == dim else 1 for axis in range(len(extent))])
    return gain


def deal_out(own_key, own, number, rows, amount, top, limit, slope):
    sequence = jax.random.permutation(own_key, amount)
    heavy_load, usual = load_shares(amount, rows * top, limit, slope, True), load_shares(amount, rows * top, limit, slope, False)
    places = jnp.arange(amount)

    def named(tallies, turn):
        used = int((tallies > 0).sum())
        fixed = max(1, used // 4)
        moved = fixed + (places - fixed + turn * (used - fixed)) % max(1, amount - fixed)
        return jnp.zeros((amount,), jnp.int32).at[sequence[jnp.where(places < fixed, places, moved)]].set(jnp.asarray(tallies, jnp.int32))

    tallies = jnp.where(number % 4 == 0, named(heavy_load, number // 4), named(usual, number - number // 4 - 1))
    mixed = jax.random.permutation(jax.random.fold_in(own, 3), amount)
    giver, taker = mixed[0:amount // 2 * 2:2], mixed[1:amount // 2 * 2:2]
    margin = jnp.minimum(tallies[giver] - 1, limit - tallies[taker]) // 2
    margin = jnp.where((giver == sequence[0]) | (taker == sequence[0]) | (tallies[taker] == 0), 0, jnp.maximum(margin, 0))
    moved = jax.random.randint(jax.random.fold_in(own, 4), (amount // 2,), 0, 1 << 20) % (margin + 1)
    tallies = tallies.at[giver].add(-moved).at[taker].add(moved)
    members = jnp.searchsorted(jnp.cumsum(tallies), jnp.arange(rows * top), side="right").astype(jnp.int32)
    table = members.reshape(top, rows).T
    table = table[jax.random.permutation(jax.random.fold_in(own, 1), rows)]
    turn = jax.random.randint(jax.random.fold_in(own, 2), (rows, 1), 0, top)
    return jnp.take_along_axis(table, (jnp.arange(top)[None, :] + turn) % top, axis=1)


def load_shares(count, total, bound, slope, full):
    loads = [(1 << 20) // math.isqrt(rank ** slope) + 1 for rank in range(1, count + 1)]
    largest = bound if full else min(bound, max(-(-total // count), total * loads[0] // sum(loads)))
    least = 1 if total - largest >= count - 1 else 0
    counts, spare = [largest] + [least] * (count - 1), total - largest - least * (count - 1)
    while spare > 0:
        movable = [i for i in range(1, count) if counts[i] < largest] or [i for i in range(1, count) if counts[i] < bound]
        whole, left = sum([loads[i] for i in movable]), spare
        for i in movable:
            more = min(bound - counts[i], max(1, left * loads[i] // whole), spare)
            counts[i] = counts[i] + more
            spare = spare - more
    return np.array(counts)


def gaussian(own_key, dims, scale, most, split=(), held_as=jnp.bfloat16):
    array = scale * jax.random.normal(own_key, dims, jnp.float32)
    if split:
        array = array * steps_of(own_key, dims, split, -0.22, 0.18)
    return jnp.clip(array, -most, most).astype(held_as)


def setup_inputs(seed: int = 0) -> dict:
    streams_of = jax.random.split(jax.random.key(seed), 13)
    basis = draw_basis(jax.random.fold_in(streams_of[12], 71), 0)
    interface_row_owner_keys = jax.random.split(jax.random.fold_in(streams_of[1], 1), TOTAL_SLOTS // BOUNDARY_SLOTS)
    interface_row_owner_turns = jax.random.permutation(jax.random.fold_in(streams_of[1], 3), TOTAL_SLOTS // BOUNDARY_SLOTS)
    interface_row_owner = jax.vmap(lambda own, number: deal_out(jax.random.fold_in(streams_of[1], 2), own, number, BOUNDARY_SLOTS, DEVICES, 1, SUBDOMAIN_SLOTS, 2))(interface_row_owner_keys, interface_row_owner_turns).reshape((TOTAL_SLOTS, 1))
    interface_local_row = touch_ends(jax.random.randint(streams_of[2], (TOTAL_SLOTS,), 0, ROWS_PER_OWNER), jax.random.fold_in(streams_of[2], 1), 0, ROWS_PER_OWNER - 1).astype(jnp.int32)
    interface_slot_weight = jnp.clip(0.25 + 0.75 * jax.random.uniform(streams_of[3], (TOTAL_SLOTS,), jnp.float32) ** steps_of(streams_of[3], (TOTAL_SLOTS,), ((0, 128),), -0.2, 0.2), 0.25, 1.0)
    local_inverse = draw_local_inverse(jax.random.fold_in(streams_of[12], 71), 0)
    prim_index = touch_ends(jax.random.randint(streams_of[5], (DEVICES * NPRIM,), 0, BOUNDARY_SLOTS), jax.random.fold_in(streams_of[5], 1), 0, BOUNDARY_SLOTS - 1).astype(jnp.int32)
    prim_vector = gaussian(streams_of[6], (BLOCK_REALS, DEVICES * NPRIM), 0.3, 4.0, ((1, 128),), jnp.float32)
    coarse_inverse = gaussian(streams_of[7], (NCS, NCS), NCS ** -0.5, 0.1875, ((0, 32),), jnp.float32)
    interface_shifted_diagonal = jnp.clip(2.0 + 2.0 * jax.random.uniform(streams_of[8], (BLOCK_REALS, TOTAL_SLOTS), jnp.float32) ** steps_of(streams_of[8], (BLOCK_REALS, TOTAL_SLOTS), ((1, 128),), -0.2, 0.2), 2.0, 4.0)
    coupling_index = touch_ends(jax.random.randint(streams_of[9], (KC, NINT), 0, BOUNDARY_SLOTS), jax.random.fold_in(streams_of[9], 1), 0, BOUNDARY_SLOTS - 1).astype(jnp.int32)
    coupling_blocks = gaussian(streams_of[10], (KC, BLOCK_REALS, BLOCK_REALS, NINT), BLOCK_REALS ** -0.5, 0.75, ((3, 128),))
    interior_inverse = draw_interior_inverse(jax.random.fold_in(streams_of[12], 71), 0)
    return dict(basis=basis, interface_row_owner=interface_row_owner, interface_local_row=interface_local_row, interface_slot_weight=interface_slot_weight, local_inverse=local_inverse, prim_index=prim_index, prim_vector=prim_vector, coarse_inverse=coarse_inverse, interface_shifted_diagonal=interface_shifted_diagonal, coupling_index=coupling_index, coupling_blocks=coupling_blocks, interior_inverse=interior_inverse)


HIGH = lax.Precision.HIGHEST

def reference(basis, interface_row_owner, interface_local_row, interface_slot_weight, local_inverse, prim_index, prim_vector, coarse_inverse, interface_shifted_diagonal, coupling_index, coupling_blocks, interior_inverse):
    row_of = (interface_row_owner[:, 0] * ROWS_PER_OWNER + interface_local_row).astype(jnp.int32)
    prim_slot = (jnp.arange(DEVICES * NPRIM, dtype=jnp.int32) // NPRIM * BOUNDARY_SLOTS + prim_index).astype(jnp.int32)
    vector = basis[KB - 1]
    restricted = vector[:, row_of] * interface_slot_weight[None, :]
    owner_devices = jnp.arange(DEVICES, dtype=jnp.int32)

    def neumann_solve(device_id):
        blocks_here = lax.dynamic_slice_in_dim(local_inverse, device_id * BOUNDARY_SLOTS, BOUNDARY_SLOTS, 2).astype(jnp.float32)
        piece_here = lax.dynamic_slice_in_dim(restricted, device_id * BOUNDARY_SLOTS, BOUNDARY_SLOTS, 1)
        return jnp.einsum('abj,bj->aj', blocks_here, piece_here, precision=HIGH)
    neumann_piece = jnp.transpose(lax.map(neumann_solve, owner_devices), (1, 0, 2)).reshape(BLOCK_REALS, TOTAL_SLOTS)
    contrib = lax.optimization_barrier(jnp.sum(prim_vector * restricted[:, prim_slot], axis=0))
    coarse_rhs = contrib.reshape(N_STREAM, N_SPAN, NPRIM).sum(axis=1).reshape(NCS)
    coarse_sol = jnp.dot(coarse_inverse, coarse_rhs, precision=HIGH)
    spread = jnp.broadcast_to(coarse_sol.reshape(N_STREAM, 1, NPRIM), (N_STREAM, N_SPAN, NPRIM)).reshape(DEVICES * NPRIM)
    corrected = neumann_piece.at[:, prim_slot].add(spread[None, :] * prim_vector)
    assembled = jnp.zeros((BLOCK_REALS, NG), jnp.float32).at[:, row_of].add(corrected * interface_slot_weight[None, :])
    restored = assembled[:, row_of]

    def apply_schur_complement(device_id):
        blocks_here = lax.dynamic_slice_in_dim(coupling_blocks, device_id * NIN, NIN, 3).astype(jnp.float32)
        inverse_here = lax.dynamic_slice_in_dim(interior_inverse, device_id * NIN, NIN, 2).astype(jnp.float32)
        index_here = lax.dynamic_slice_in_dim(coupling_index, device_id * NIN, NIN, 1).astype(jnp.int32)
        piece_here = lax.dynamic_slice_in_dim(restored, device_id * BOUNDARY_SLOTS, BOUNDARY_SLOTS, 1)
        diagonal_here = lax.dynamic_slice_in_dim(interface_shifted_diagonal, device_id * BOUNDARY_SLOTS, BOUNDARY_SLOTS, 1)
        gathered = piece_here[:, index_here]
        interior_in = jnp.einsum('kabi,bki->ai', blocks_here, gathered, precision=HIGH)
        interior_sol = jnp.einsum('abi,bi->ai', inverse_here, interior_in, precision=HIGH)
        backward = jnp.einsum('kabi,ai->bki', blocks_here, interior_sol, precision=HIGH)
        folded = jnp.zeros((BLOCK_REALS, BOUNDARY_SLOTS), jnp.float32).at[:, index_here].add(backward)
        return diagonal_here * piece_here - folded
    subdomain_image = jnp.transpose(lax.map(apply_schur_complement, owner_devices), (1, 0, 2)).reshape(BLOCK_REALS, TOTAL_SLOTS)
    image = jnp.zeros((BLOCK_REALS, NG), jnp.float32).at[:, row_of].add(subdomain_image)
    entries = BLOCK_REALS * NG
    inv_root = 1.0 / math.sqrt(entries)
    projected = lax.optimization_barrier(jnp.sum(basis * image[None], axis=(1, 2))) * inv_root
    remainder = image - jnp.einsum('k,kar->ar', projected, basis, precision=HIGH) * inv_root
    root_mean = jnp.sqrt(jnp.sum(remainder * remainder) / entries + 1e-06)
    return (remainder / root_mean, jnp.concatenate([projected, root_mean[None]]))
```

```python
import math

import jax
import jax.numpy as jnp
from jax import lax
from jax.sharding import PartitionSpec as P

HIGH = lax.Precision.HIGHEST


def body(
    basis,
    interface_row_owner,
    interface_local_row,
    interface_slot_weight,
    local_inverse,
    prim_index,
    prim_vector,
    coarse_inverse,
    interface_shifted_diagonal,
    coupling_index,
    coupling_blocks,
    interior_inverse,
):
    stream_count = lax.axis_size("stream")
    span_count = lax.axis_size("span")
    devices = stream_count * span_count
    width = basis.shape[1]
    rows_dev = basis.shape[2]
    slots = interface_local_row.shape[0]
    capacity = 2 * ((slots + devices - 1) // devices)
    owners = interface_row_owner[:, 0]
    one_hot = (owners[:, None] == jnp.arange(devices, dtype=jnp.int32)[None, :]).astype(jnp.int32)
    earlier = jnp.cumsum(one_hot, axis=0) - one_hot
    ranking = jnp.sum(earlier * one_hot, axis=1)
    placed = owners * capacity + ranking
    requests = jnp.zeros((devices * capacity,), jnp.int32).at[placed].set(interface_local_row)
    asked = lax.all_to_all(
        requests.reshape(devices, capacity),
        ("stream", "span"),
        split_axis=0,
        concat_axis=0,
        tiled=True,
    ).reshape(devices * capacity)

    def relayout(buffer):
        return lax.all_to_all(buffer, ("stream", "span"), split_axis=0, concat_axis=0, tiled=True)

    def everywhere(values):
        copies = jnp.broadcast_to(values[None, None, :], (devices, 1, values.shape[0]))
        return relayout(copies)[:, 0, :]

    def fetch_rows(owned_field):
        fetched = owned_field.T[asked]
        arrived = relayout(fetched.reshape(devices, capacity * width))
        return arrived.reshape(devices * capacity, width)[placed].T

    def deposit(values):
        buffer = jnp.zeros((devices * capacity, width), jnp.float32).at[placed].set(values.T)
        arrived = relayout(buffer.reshape(devices, capacity * width)).reshape(
            devices * capacity, width
        )
        return jnp.zeros((rows_dev, width), jnp.float32).at[asked].add(arrived).T

    vector = basis[basis.shape[0] - 1]
    restricted = fetch_rows(vector) * interface_slot_weight[None, :]
    neumann_piece = jnp.sum(local_inverse * restricted[None, :, :], axis=1)
    contrib = jnp.sum(prim_vector * restricted[:, prim_index], axis=0)
    nprim = contrib.shape[0]
    coarse_rhs = jnp.sum(everywhere(contrib).reshape(stream_count, span_count, nprim), axis=1).reshape(
        stream_count * nprim
    )
    coarse_sol = jnp.dot(coarse_inverse, coarse_rhs, precision=HIGH)
    corrected = neumann_piece.at[:, prim_index].add(coarse_sol[None, :] * prim_vector)
    assembled = deposit(corrected * interface_slot_weight[None, :])
    restored = fetch_rows(assembled)
    gathered = jnp.transpose(restored[:, coupling_index], (1, 0, 2))
    interior_in = jnp.sum(coupling_blocks * gathered[:, None, :, :], axis=(0, 2))
    interior_sol = jnp.sum(interior_inverse * interior_in[None, :, :], axis=1)
    backward = jnp.transpose(
        jnp.sum(coupling_blocks * interior_sol[None, :, None, :], axis=1), (1, 0, 2)
    )
    folded = jnp.zeros(restored.shape, jnp.float32).at[:, coupling_index].add(backward)
    subdomain_image = interface_shifted_diagonal * restored - folded
    image = deposit(subdomain_image)
    entries = width * rows_dev * devices
    inv_root = 1.0 / math.sqrt(entries)
    kb = basis.shape[0]
    stats = [jnp.sum(image * image)[None], jnp.sum(basis * image[None], axis=(1, 2))]
    stats += [jnp.sum(basis[k][None] * basis[k:], axis=(1, 2)) for k in range(kb)]
    totals = jnp.sum(everywhere(jnp.concatenate(stats)), axis=0)
    projected = totals[1 : 1 + kb] * inv_root
    remainder = image - jnp.einsum("k,kar->ar", projected, basis, precision=HIGH) * inv_root
    step = projected * inv_root
    quad = jnp.float32(0)
    at = 1 + kb
    for k in range(kb):
        for other in range(k, kb):
            quad = quad + (1.0 if other == k else 2.0) * step[k] * step[other] * totals[at]
            at += 1
    expanded = totals[0] - 2.0 * jnp.sum(step * totals[1 : 1 + kb]) + quad
    squares = lax.cond(
        expanded > 0.01 * totals[0],
        lambda: expanded,
        lambda: jnp.sum(everywhere(jnp.sum(remainder * remainder)[None])),
    )
    root_mean = jnp.sqrt(squares / entries + 1e-06)
    return (remainder / root_mean, jnp.concatenate([projected, root_mean[None]]))


def solution(mesh):
    placed = (
        P(None, None, ("stream", "span")),
        P(("stream", "span"), None),
        P(("stream", "span")),
        P(("stream", "span")),
        P(None, None, ("stream", "span")),
        P(("stream", "span")),
        P(None, ("stream", "span")),
        P("stream", None),
        P(None, ("stream", "span")),
        P(None, ("stream", "span")),
        P(None, None, None, ("stream", "span")),
        P(None, None, ("stream", "span")),
    )
    return jax.shard_map(
        body,
        mesh=mesh,
        in_specs=placed,
        out_specs=(P(None, ("stream", "span")), P()),
        check_vma=False,
    )
```

```python
import functools
import math

import jax
import jax.numpy as jnp
from jax import lax
from jax.experimental import pallas as pl
from jax.experimental.pallas import tpu as pltpu
from jax.sharding import PartitionSpec as P

HIGH = lax.Precision.HIGHEST
F32 = jnp.float32
BF16 = jnp.bfloat16
LANES = 128
PAIRS = 8


def split(x):
    high = x.astype(BF16)
    return high, (x - high.astype(F32)).astype(BF16)


def mm(a, b):
    return jnp.dot(a, b, preferred_element_type=F32)


def mm_nt(a, b, precision=None):
    return lax.dot_general(a, b, (((1,), (1,)), ((), ())), precision=precision, preferred_element_type=F32)


def one_hot(mask):
    return jnp.where(mask, 1.0, 0.0).astype(BF16)


def message_rows(k, count):
    return pl.ds(k, count, stride=PAIRS)


def call(kernel, out_shape, *args, vmem=16, **kw):
    return pl.pallas_call(
        kernel,
        out_shape=out_shape,
        compiler_params=pltpu.CompilerParams(vmem_limit_bytes=vmem * 1024 * 1024),
        **kw,
    )(*args)


def plan_kernel(owner_ref, row_ref, request_ref, rank_ref):
    slots = owner_ref.shape[1]
    devices = request_ref.shape[0]
    owner = owner_ref[...]
    row = row_ref[...]
    named = one_hot(lax.broadcasted_iota(jnp.int32, (devices, slots), 0) == owner)
    before = lax.broadcasted_iota(jnp.int32, (LANES, LANES), 0) < lax.broadcasted_iota(
        jnp.int32, (LANES, LANES), 1
    )
    counter = jnp.concatenate([one_hot(before), jnp.ones((LANES, LANES), BF16)], axis=1)
    carry = jnp.zeros((devices, LANES), F32)
    ranks = []
    for block in range(slots // LANES):
        part = named[:, block * LANES : (block + 1) * LANES]
        counts = mm(part, counter)
        ranks.append(jnp.sum((counts[:, :LANES] + carry) * part.astype(F32), axis=0, keepdims=True))
        carry = carry + counts[:, LANES:]
    rank = jnp.concatenate(ranks, axis=1).astype(jnp.int32)
    rank_ref[...] = rank
    at_rank = lax.broadcasted_iota(jnp.int32, (LANES, slots), 0) == rank
    tens = jnp.where(at_rank, (row >> 4).astype(F32), 0.0).astype(BF16)
    units = jnp.where(at_rank, (row & 15).astype(F32), 0.0).astype(BF16)
    request_ref[...] = (16.0 * mm_nt(named, tens) + mm_nt(named, units)).astype(jnp.int32)


def slots_from_messages(message_ref, owner, rank):
    slots = owner.shape[1]
    devices = message_ref.shape[0] // PAIRS
    width = LANES // 2
    sides = []
    for k in range(PAIRS):
        high, low = split(message_ref[message_rows(k, devices), :].T)
        sides.append(jnp.concatenate([high, low], axis=1))
    chunk = 256
    pieces = []
    for c in range(slots // chunk):
        lanes = slice(c * chunk, (c + 1) * chunk)
        named = one_hot(lax.broadcasted_iota(jnp.int32, (devices, chunk), 0) == owner[:, lanes])
        named = jnp.concatenate([named, named], axis=0)
        place = jnp.broadcast_to(rank[:, lanes], (width, chunk))
        total = jnp.zeros((width, chunk), F32)
        for k in range(PAIRS):
            both = mm(sides[k], named)
            total = jnp.where(place == 2 * k, both[:width], total)
            total = jnp.where(place == 2 * k + 1, both[width:], total)
        pieces.append(total)
    return jnp.concatenate(pieces, axis=1)


def slots_to_messages(values, owner, rank, message_ref):
    slots = owner.shape[1]
    devices = message_ref.shape[0] // PAIRS
    high, low = split(values)
    named = one_hot(lax.broadcasted_iota(jnp.int32, (devices, slots), 0) == owner)
    for k in range(PAIRS):
        first = one_hot(rank == 2 * k)
        second = one_hot(rank == 2 * k + 1)
        placed = jnp.concatenate([high * first, high * second, low * first, low * second], axis=0)
        both = mm_nt(named, placed)
        message_ref[message_rows(k, devices), :] = both[:, :LANES] + both[:, LANES:]


def restrict_kernel(message_ref, owner_ref, rank_ref, weight_ref, prim_ref, vector_ref, out_ref, contrib_ref):
    slots = owner_ref.shape[1]
    restricted = slots_from_messages(message_ref, owner_ref[...], rank_ref[...]) * weight_ref[...]
    out_ref[...] = restricted
    nprim = prim_ref.shape[0]
    chosen = jnp.where(
        lax.broadcasted_iota(jnp.int32, (nprim, slots), 1) == prim_ref[...], 1.0, 0.0
    )
    at_prim = mm_nt(restricted, chosen, HIGH)
    contrib = jnp.sum(at_prim * vector_ref[...], axis=0, keepdims=True)
    wide = jnp.concatenate([contrib, jnp.zeros((1, LANES - nprim), F32)], axis=1)
    contrib_ref[...] = jnp.broadcast_to(wide, contrib_ref.shape)


def correct_kernel(
    neumann_ref, gathered_ref, inverse_ref, owner_ref, rank_ref, weight_ref, prim_ref, vector_ref, message_ref, *, span
):
    slots = owner_ref.shape[1]
    nprim = prim_ref.shape[0]
    devices = gathered_ref.shape[0]
    streams = devices // span
    ncs = inverse_ref.shape[1]
    contrib = gathered_ref[...][:, :nprim]
    lane = lax.broadcasted_iota(jnp.int32, (nprim, ncs), 1)
    spread = jnp.where(lax.rem(lane, nprim) == lax.broadcasted_iota(jnp.int32, (nprim, ncs), 0), 1.0, 0.0)
    tiled = jnp.dot(contrib, spread, precision=HIGH, preferred_element_type=F32)
    device = lax.broadcasted_iota(jnp.int32, (devices, ncs), 0)
    stream = lax.broadcasted_iota(jnp.int32, (devices, ncs), 1)
    mine = lax.div(device, span) == lax.div(stream, nprim)
    coarse_rhs = jnp.sum(jnp.where(mine, tiled, 0.0), axis=0, keepdims=True)
    coarse_sol = jnp.sum(inverse_ref[...] * coarse_rhs, axis=1, keepdims=True)
    chosen = jnp.where(
        lax.broadcasted_iota(jnp.int32, (nprim, slots), 1) == prim_ref[...], coarse_sol, 0.0
    )
    correction = jnp.dot(vector_ref[...], chosen, precision=HIGH, preferred_element_type=F32)
    corrected = (neumann_ref[...] + correction) * weight_ref[...]
    slots_to_messages(corrected, owner_ref[...], rank_ref[...], message_ref)


def restore_kernel(message_ref, owner_ref, rank_ref, index_ref, out_ref, gathered_ref):
    restored = slots_from_messages(message_ref, owner_ref[...], rank_ref[...])
    out_ref[...] = restored
    width, slots = restored.shape
    kc, inner = index_ref.shape
    both = jnp.concatenate(split(restored), axis=0)
    for k in range(kc):
        chosen = one_hot(lax.broadcasted_iota(jnp.int32, (slots, inner), 0) == index_ref[k : k + 1, :])
        got = mm(both, chosen)
        gathered_ref[k] = got[:width] + got[width:]


def image_kernel(backward_ref, restored_ref, diagonal_ref, owner_ref, rank_ref, index_ref, message_ref):
    width, slots = restored_ref.shape
    kc, inner = index_ref.shape
    value = diagonal_ref[...] * restored_ref[...]
    for k in range(kc):
        both = jnp.concatenate(split(backward_ref[k]), axis=0)
        chosen = one_hot(lax.broadcasted_iota(jnp.int32, (slots, inner), 0) == index_ref[k : k + 1, :])
        got = mm_nt(both, chosen)
        value = value - (got[:width] + got[width:])
    slots_to_messages(value, owner_ref[...], rank_ref[...], message_ref)


def rows_to_messages(values, asked, message_ref):
    width, rows = values.shape
    devices = asked.shape[1]
    both = jnp.concatenate(split(values), axis=0)
    place = lax.broadcasted_iota(jnp.int32, (rows, devices), 0)
    for k in range(PAIRS):
        chosen = jnp.concatenate(
            [one_hot(place == asked[2 * k : 2 * k + 1]), one_hot(place == asked[2 * k + 1 : 2 * k + 2])], axis=1
        )
        got = mm(both, chosen)
        got = got[:width] + got[width:]
        stacked = jnp.concatenate([got[:, :devices], got[:, devices:]], axis=0)
        message_ref[message_rows(k, devices), :] = stacked.T


def rows_from_messages(message_ref, asked, rows):
    devices = asked.shape[1]
    width = LANES // 2
    place = lax.broadcasted_iota(jnp.int32, (rows, devices), 0)
    totals = [jnp.zeros((rows, 2 * LANES), F32), jnp.zeros((rows, 2 * LANES), F32)]
    for k in range(0, PAIRS, 2):
        parts = []
        for step in (k, k + 1):
            parts.append(jnp.concatenate(split(message_ref[message_rows(step, devices), :]), axis=1))
        parts = jnp.concatenate(parts, axis=0)
        for side in range(2):
            a, b = 2 * k + side, 2 * k + 2 + side
            chosen = jnp.concatenate(
                [one_hot(place == asked[a : a + 1]), one_hot(place == asked[b : b + 1])], axis=1
            )
            totals[side] = totals[side] + mm(chosen, parts)
    sides = [t[:, :LANES] + t[:, LANES:] for t in totals]
    lane = lax.broadcasted_iota(jnp.int32, (rows, LANES), 1)
    both = jnp.where(lane < width, sides[0], sides[1]).T
    return both[:width] + both[width:]


def fetch_kernel(request_ref, vector_ref, asked_ref, message_ref):
    asked = request_ref[...].astype(F32).T.astype(jnp.int32)[: 2 * PAIRS]
    asked_ref[...] = asked
    rows_to_messages(vector_ref[...], asked, message_ref)


def assemble_kernel(arrived_ref, asked_ref, message_ref, *, rows):
    asked = asked_ref[...]
    assembled = rows_from_messages(arrived_ref, asked, rows)
    rows_to_messages(assembled, asked, message_ref)


def two_sum(a, b):
    total = a + b
    back = total - a
    return total, (a - (total - back)) + (b - back)


def pair_add(a, b):
    total, rest = two_sum(a[0], b[0])
    return total, rest + (a[1] + b[1])


def final_kernel(arrived_ref, asked_ref, basis_ref, image_ref, stats_ref):
    kb, width, rows = basis_ref.shape
    image = rows_from_messages(arrived_ref, asked_ref[...], rows)
    image_ref[...] = image
    fields = [image] + [basis_ref[k] for k in range(kb)]
    quantities = []
    for i in range(1 + kb):
        for j in range(i, 1 + kb):
            product = fields[i] * fields[j]
            pair = (jnp.zeros((8, LANES), F32), jnp.zeros((8, LANES), F32))
            for a in range(0, width, 8):
                for b in range(0, rows, LANES):
                    total, rest = two_sum(pair[0], product[a : a + 8, b : b + LANES])
                    pair = (total, pair[1] + rest)
            for shift in (4, 2, 1):
                pair = pair_add(pair, tuple(pltpu.roll(p, shift, 0) for p in pair))
            quantities.append(pair)
    row = lax.broadcasted_iota(jnp.int32, (8, LANES), 0)
    tiles = []
    for base in range(0, len(quantities), 8):
        tile = (jnp.zeros((8, LANES), F32), jnp.zeros((8, LANES), F32))
        for n, pair in enumerate(quantities[base : base + 8]):
            tile = tuple(jnp.where(row == n, p, t) for p, t in zip(pair, tile))
        shift = LANES // 2
        while shift:
            tile = pair_add(tile, tuple(pltpu.roll(t, shift, 1) for t in tile))
            shift //= 2
        tiles.append(tile)
    pad = [jnp.zeros((LANES - 16 * len(tiles), LANES), F32)]
    square = jnp.concatenate([t[0] for t in tiles] + [t[1] for t in tiles] + pad, axis=0)
    stats_ref[...] = square.T


def finish_kernel(gathered_ref, image_ref, basis_ref, direction_ref, coeff_ref, *, entries):
    kb = basis_ref.shape[0]
    devices = gathered_ref.shape[0]
    count = (kb + 1) * (kb + 2) // 2
    tiles = -(-count // 8)
    values = gathered_ref[...]
    high = values
    low = pltpu.roll(values, LANES - 8 * tiles, 1)
    half = devices // 2
    pair = (high, low)
    while half >= 1:
        pair = pair_add(
            tuple(p[:half] for p in pair), tuple(p[half : 2 * half] for p in pair)
        )
        half //= 2
    lane = lax.broadcasted_iota(jnp.int32, (1, LANES), 1)

    def entry(n):
        return tuple(jnp.sum(jnp.where(lane == n, p, 0.0), axis=1, keepdims=True) for p in pair)

    numbers = [entry(n) for n in range(count)]
    inv_root = 1.0 / math.sqrt(entries)
    projected = [(numbers[1 + k][0] + numbers[1 + k][1]) * inv_root for k in range(kb)]
    steps = [p * inv_root for p in projected]

    def add_product(total, factor, number):
        a, b = factor, number[0]
        a_high = a * 4097.0
        a_high = a_high - (a_high - a)
        b_high = b * 4097.0
        b_high = b_high - (b_high - b)
        a_low, b_low = a - a_high, b - b_high
        product = a * b
        rest = ((a_high * b_high - product) + a_high * b_low + a_low * b_high) + a_low * b_low
        return pair_add(total, (product, rest + factor * number[1]))

    def scaled(number, factor):
        zero = jnp.zeros_like(factor)
        return add_product((zero, zero), factor, number)

    total = numbers[0]
    at = 1 + kb
    for k in range(kb):
        total = add_product(total, -2.0 * steps[k], numbers[1 + k])
    for k in range(kb):
        for other in range(k, kb):
            factor = steps[k] if other == k else 2.0 * steps[k]
            total = add_product(total, factor, scaled(numbers[at], steps[other]))
            at += 1
    squares = jnp.maximum(total[0] + total[1], 0.0)
    root_mean = jnp.sqrt(squares / entries + 1e-06)
    remainder = image_ref[...]
    for k in range(kb):
        remainder = remainder - steps[k] * basis_ref[k]
    direction_ref[...] = remainder / root_mean
    coeffs = jnp.zeros((1, LANES), F32)
    for n, value in enumerate(projected + [root_mean]):
        coeffs = jnp.where(lane == n, value, coeffs)
    coeff_ref[...] = coeffs


def body(
    basis,
    interface_row_owner,
    interface_local_row,
    interface_slot_weight,
    local_inverse,
    prim_index,
    prim_vector,
    coarse_inverse,
    interface_shifted_diagonal,
    coupling_index,
    coupling_blocks,
    interior_inverse,
):
    span = lax.axis_size("span")
    devices = lax.axis_size("stream") * span
    kb, width, rows = basis.shape
    slots = interface_local_row.shape[0]
    kc, inner = coupling_index.shape
    nprim = prim_index.shape[0]
    entries = width * rows * devices
    owner = interface_row_owner.reshape(1, slots)
    row = interface_local_row.reshape(1, slots)
    weight = interface_slot_weight.reshape(1, slots)
    prim = prim_index.reshape(nprim, 1)
    shape = jax.ShapeDtypeStruct
    message = shape((devices * PAIRS, LANES), F32)
    field = shape((width, slots), F32)
    square = shape((devices, LANES), F32)

    def exchange(x, per):
        sent = x.reshape(devices, per, LANES)
        return lax.all_to_all(sent, ("stream", "span"), split_axis=0, concat_axis=0, tiled=True).reshape(x.shape)

    requests, rank = call(
        plan_kernel, (shape((devices, LANES), jnp.int32), shape((1, slots), jnp.int32)), owner, row
    )
    arrived = exchange(requests, 1)
    asked, sent = call(fetch_kernel, (shape((2 * PAIRS, devices), jnp.int32), message), arrived, basis[kb - 1])
    restricted, contrib = call(
        restrict_kernel, (field, square), exchange(sent, PAIRS), owner, rank, weight, prim, prim_vector
    )
    contribs = exchange(contrib, 1)
    neumann_piece = jnp.sum(local_inverse * restricted[None, :, :], axis=1)
    sent = call(
        functools.partial(correct_kernel, span=span),
        message,
        neumann_piece,
        contribs,
        coarse_inverse,
        owner,
        rank,
        weight,
        prim,
        prim_vector,
    )
    sent = call(functools.partial(assemble_kernel, rows=rows), message, exchange(sent, PAIRS), asked)
    restored, gathered = call(
        restore_kernel,
        (field, shape((kc, width, inner), F32)),
        exchange(sent, PAIRS),
        owner,
        rank,
        coupling_index,
    )
    interior_in = jnp.sum(coupling_blocks * gathered[:, None, :, :], axis=(0, 2))
    interior_sol = jnp.sum(interior_inverse * interior_in[None, :, :], axis=1)
    backward = jnp.sum(coupling_blocks * interior_sol[None, :, None, :], axis=1)
    sent = call(
        image_kernel,
        message,
        backward,
        restored,
        interface_shifted_diagonal,
        owner,
        rank,
        coupling_index,
    )
    image, stats = call(
        final_kernel, (shape((width, rows), F32), square), exchange(sent, PAIRS), asked, basis
    )
    direction, coeffs = call(
        functools.partial(finish_kernel, entries=entries),
        (shape((width, rows), F32), shape((1, LANES), F32)),
        exchange(stats, 1),
        image,
        basis,
    )
    return direction, coeffs[0, : kb + 1]


def solution(mesh):
    placed = (
        P(None, None, ("stream", "span")),
        P(("stream", "span"), None),
        P(("stream", "span")),
        P(("stream", "span")),
        P(None, None, ("stream", "span")),
        P(("stream", "span")),
        P(None, ("stream", "span")),
        P("stream", None),
        P(None, ("stream", "span")),
        P(None, ("stream", "span")),
        P(None, None, None, ("stream", "span")),
        P(None, None, ("stream", "span")),
    )
    return jax.shard_map(
        body,
        mesh=mesh,
        in_specs=placed,
        out_specs=(P(None, ("stream", "span")), P()),
        check_vma=False,
    )
```

```python
import functools
import math

import jax
import jax.numpy as jnp
from jax import lax
from jax.experimental import pallas as pl
from jax.experimental.pallas import tpu as pltpu
from jax.sharding import PartitionSpec as P

HIGH = lax.Precision.HIGHEST
F32 = jnp.float32
BF16 = jnp.bfloat16
LANES = 128
PAIRS = 8


def split(x):
    high = x.astype(BF16)
    return high, (x - high.astype(F32)).astype(BF16)


def mm(a, b):
    return jnp.dot(a, b, preferred_element_type=F32)


def mm_nt(a, b, precision=None):
    return lax.dot_general(a, b, (((1,), (1,)), ((), ())), precision=precision, preferred_element_type=F32)


def one_hot(mask):
    return jnp.where(mask, 1.0, 0.0).astype(BF16)


def message_rows(k, count):
    return pl.ds(k, count, stride=PAIRS)


def call(kernel, out_shape, *args, vmem=16, **kw):
    return pl.pallas_call(
        kernel,
        out_shape=out_shape,
        compiler_params=pltpu.CompilerParams(vmem_limit_bytes=vmem * 1024 * 1024),
        **kw,
    )(*args)


def plan_kernel(owner_hbm, row_hbm, request_ref, ids_ref, owner_ref, row_ref, sems):
    slots = owner_ref.shape[1]
    devices = request_ref.shape[0]
    copies = [
        pltpu.make_async_copy(owner_hbm, owner_ref, sems.at[0]),
        pltpu.make_async_copy(row_hbm, row_ref, sems.at[1]),
    ]
    for copy in copies:
        copy.start()
    for copy in copies:
        copy.wait()
    owner = owner_ref[...]
    row = row_ref[...]
    named = one_hot(lax.broadcasted_iota(jnp.int32, (devices, slots), 0) == owner)
    before = lax.broadcasted_iota(jnp.int32, (LANES, LANES), 0) < lax.broadcasted_iota(
        jnp.int32, (LANES, LANES), 1
    )
    counter = jnp.concatenate([one_hot(before), jnp.ones((LANES, LANES), BF16)], axis=1)
    carry = jnp.zeros((devices, LANES), F32)
    ranks = []
    for block in range(slots // LANES):
        part = named[:, block * LANES : (block + 1) * LANES]
        counts = mm(part, counter)
        ranks.append(jnp.sum((counts[:, :LANES] + carry) * part.astype(F32), axis=0, keepdims=True))
        carry = carry + counts[:, LANES:]
    rank = jnp.concatenate(ranks, axis=1).astype(jnp.int32)
    ids_ref[0:1, :] = owner
    ids_ref[1:2, :] = rank
    at_rank = lax.broadcasted_iota(jnp.int32, (LANES, slots), 0) == rank
    tens = jnp.where(at_rank, (row >> 4).astype(F32), 0.0).astype(BF16)
    units = jnp.where(at_rank, (row & 15).astype(F32), 0.0).astype(BF16)
    request_ref[...] = (16.0 * mm_nt(named, tens) + mm_nt(named, units)).astype(jnp.int32)


def slots_from_messages(message_ref, owner, rank):
    slots = owner.shape[1]
    devices = message_ref.shape[0] // PAIRS
    width = LANES // 2
    sides = []
    for k in range(PAIRS):
        high, low = split(message_ref[message_rows(k, devices), :].T)
        sides.append(jnp.concatenate([high, low], axis=1))
    chunk = 256
    pieces = []
    for c in range(slots // chunk):
        lanes = slice(c * chunk, (c + 1) * chunk)
        named = one_hot(lax.broadcasted_iota(jnp.int32, (devices, chunk), 0) == owner[:, lanes])
        named = jnp.concatenate([named, named], axis=0)
        place = jnp.broadcast_to(rank[:, lanes], (width, chunk))
        total = jnp.zeros((width, chunk), F32)
        for k in range(PAIRS):
            both = mm(sides[k], named)
            total = jnp.where(place == 2 * k, both[:width], total)
            total = jnp.where(place == 2 * k + 1, both[width:], total)
        pieces.append(total)
    return jnp.concatenate(pieces, axis=1)


def slots_to_messages(values, owner, rank, message_ref):
    slots = owner.shape[1]
    devices = message_ref.shape[0] // PAIRS
    high, low = split(values)
    named = one_hot(lax.broadcasted_iota(jnp.int32, (devices, slots), 0) == owner)
    for k in range(PAIRS):
        first = one_hot(rank == 2 * k)
        second = one_hot(rank == 2 * k + 1)
        placed = jnp.concatenate([high * first, high * second, low * first, low * second], axis=0)
        both = mm_nt(named, placed)
        message_ref[message_rows(k, devices), :] = both[:, :LANES] + both[:, LANES:]


def block_sums(block_refs, vectors, a, lanes):
    total = None
    for ref, vector in zip(block_refs, vectors):
        product = ref[a, :, lanes].astype(F32) * vector
        part = jnp.sum(product.reshape(product.shape[0] // 8, 8, LANES), axis=0)
        total = part if total is None else total + part
    for shift in (4, 2, 1):
        total = total + pltpu.roll(total, shift, 0)
    return total


def apply_blocks(block_refs, vector_refs, out_ref, c):
    width = out_ref.shape[0]
    row = lax.broadcasted_iota(jnp.int32, (8, LANES), 0)
    lanes = slice(c * LANES, (c + 1) * LANES)
    vectors = [ref[:, lanes] for ref in vector_refs]

    def rows_of(tile, _):
        first = pl.multiple_of(tile * 8, 8)
        result = jnp.zeros((8, LANES), F32)
        for j in range(8):
            result = jnp.where(row == j, block_sums(block_refs, vectors, first + j, lanes), result)
        out_ref[pl.ds(first, 8), lanes] = result
        return 0

    lax.fori_loop(0, width // 8, rows_of, 0)


def prepare_kernel(
    ids_ref,
    weight_ref,
    prim_ref,
    vector_ref,
    basis_ref,
    weights_ref,
    chosen_ref,
    vectors_ref,
    coarse_ref,
    named_ref,
    gram_ref,
    last_ref,
):
    slots = ids_ref.shape[1]
    nprim = prim_ref.shape[0]
    devices = named_ref.shape[0]
    chosen = lax.broadcasted_iota(jnp.int32, (nprim, slots), 1) == prim_ref[...]
    weights_ref[...] = weight_ref[...]
    chosen_ref[...] = jnp.where(chosen, 1.0, 0.0)
    vectors_ref[...] = vector_ref[...]

    def column(values):
        return jnp.sum(jnp.where(chosen, values.astype(F32), 0.0), axis=1, keepdims=True)

    weight, rank, owner = column(weight_ref[...]), column(ids_ref[1:2, :]), column(ids_ref[0:1, :])
    named_ref[...] = one_hot(
        lax.broadcasted_iota(jnp.int32, (nprim, devices), 1).astype(F32) == owner
    ).astype(F32).T.astype(BF16)
    vectors = vector_ref[...].T * weight
    for k in range(PAIRS):
        sides = [jnp.where(rank == 2.0 * k + side, vectors, 0.0) for side in range(2)]
        coarse_ref[k * nprim : (k + 1) * nprim, :] = jnp.concatenate(sides, axis=1)
    kb = basis_ref.shape[0]
    fields = [basis_ref[k] for k in range(kb)]
    last_ref[...] = fields[kb - 1]
    store_sums([(fields[i], fields[j]) for i in range(kb) for j in range(i, kb)], gram_ref)


def restrict_kernel(message_ref, ids_ref, weight_ref, chosen_ref, vector_ref, out_ref, contrib_ref):
    restricted = slots_from_messages(message_ref, ids_ref[0:1, :], ids_ref[1:2, :]) * weight_ref[...]
    out_ref[...] = restricted
    at_prim = mm_nt(restricted, chosen_ref[...], HIGH)
    contrib = jnp.sum(at_prim * vector_ref[...], axis=0, keepdims=True)
    wide = jnp.concatenate([contrib, jnp.zeros((1, LANES - contrib.shape[1]), F32)], axis=1)
    contrib_ref[...] = jnp.broadcast_to(wide, contrib_ref.shape)


def neumann_kernel(blocks_hbm, restricted_ref, ids_ref, weight_ref, message_ref, piece_ref, blocks_ref, sems):
    columns = piece_ref.shape[1]
    copies = []
    for c in range(columns // LANES):
        lanes = pl.ds(c * LANES, LANES)
        copies.append(pltpu.make_async_copy(blocks_hbm.at[:, :, lanes], blocks_ref.at[:, :, lanes], sems.at[c]))
    for copy in copies:
        copy.start()
    for c, copy in enumerate(copies):
        copy.wait()
        apply_blocks([blocks_ref], [restricted_ref], piece_ref, c)
    slots_to_messages(piece_ref[...] * weight_ref[...], ids_ref[0:1, :], ids_ref[1:2, :], message_ref)


def correct_kernel(packed_ref, gathered_ref, inverse_ref, coarse_ref, named_ref, message_ref, *, span):
    devices, nprim = named_ref.shape
    ncs = inverse_ref.shape[1]
    contrib = gathered_ref[...][:, :nprim]
    lane = lax.broadcasted_iota(jnp.int32, (nprim, ncs), 1)
    spread = jnp.where(lax.rem(lane, nprim) == lax.broadcasted_iota(jnp.int32, (nprim, ncs), 0), 1.0, 0.0)
    tiled = jnp.dot(contrib, spread, precision=HIGH, preferred_element_type=F32)
    device = lax.broadcasted_iota(jnp.int32, (devices, ncs), 0)
    stream = lax.broadcasted_iota(jnp.int32, (devices, ncs), 1)
    mine = lax.div(device, span) == lax.div(stream, nprim)
    coarse_rhs = jnp.sum(jnp.where(mine, tiled, 0.0), axis=0, keepdims=True)
    coarse_sol = jnp.sum(inverse_ref[...] * coarse_rhs, axis=1, keepdims=True)
    for k in range(PAIRS):
        high, low = split(coarse_ref[k * nprim : (k + 1) * nprim, :] * coarse_sol)
        both = mm(named_ref[...], jnp.concatenate([high, low], axis=1))
        at = message_rows(k, devices)
        message_ref[at, :] = packed_ref[at, :] + (both[:, :LANES] + both[:, LANES:])


def schur_kernel(
    arrived_ref,
    ids_ref,
    index_ref,
    diagonal_ref,
    coupling_hbm,
    inverse_hbm,
    message_ref,
    gathered_ref,
    inner_ref,
    backward_ref,
    coupling_ref,
    inverse_ref,
    sems,
):
    kc, inner = index_ref.shape
    chunks = inner // LANES
    copies = []
    for c in range(chunks):
        lanes = pl.ds(c * LANES, LANES)
        copies.append(
            pltpu.make_async_copy(coupling_hbm.at[:, :, :, lanes], coupling_ref.at[:, :, :, lanes], sems.at[c, 0])
        )
        copies.append(
            pltpu.make_async_copy(inverse_hbm.at[:, :, lanes], inverse_ref.at[:, :, lanes], sems.at[c, 1])
        )
    for copy in copies:
        copy.start()
    owner, rank = ids_ref[0:1, :], ids_ref[1:2, :]
    restored = slots_from_messages(arrived_ref, owner, rank)
    width, slots = restored.shape
    both = jnp.concatenate(split(restored), axis=0)
    for k in range(kc):
        chosen = one_hot(lax.broadcasted_iota(jnp.int32, (slots, inner), 0) == index_ref[k : k + 1, :])
        got = mm(both, chosen)
        gathered_ref[k] = got[:width] + got[width:]
    blocks = [coupling_ref.at[k] for k in range(kc)]
    for c in range(chunks):
        for copy in copies[2 * c : 2 * c + 2]:
            copy.wait()
        apply_blocks(blocks, [gathered_ref.at[k] for k in range(kc)], inner_ref, c)
        lanes = slice(c * LANES, (c + 1) * LANES)
        vector = inner_ref[:, lanes]

        def step(tile, totals, lanes=lanes, vector=vector):
            for j in range(8):
                a = tile * 8 + j
                solved = block_sums([inverse_ref], [vector], a, lanes)
                totals = tuple(
                    total + ref[a, :, lanes].astype(F32).reshape(width // 8, 8, LANES) * solved[None]
                    for total, ref in zip(totals, blocks)
                )
            return totals

        zero = jnp.zeros((width // 8, 8, LANES), F32)
        totals = lax.fori_loop(0, width // 8, step, (zero,) * kc)
        for k in range(kc):
            backward_ref[k, :, lanes] = totals[k].reshape(width, LANES)
    value = diagonal_ref[...] * restored
    for k in range(kc):
        both = jnp.concatenate(split(backward_ref[k]), axis=0)
        chosen = one_hot(lax.broadcasted_iota(jnp.int32, (slots, inner), 0) == index_ref[k : k + 1, :])
        got = mm_nt(both, chosen)
        value = value - (got[:width] + got[width:])
    slots_to_messages(value, owner, rank, message_ref)


def rows_to_messages(values, asked, message_ref):
    width, rows = values.shape
    devices = asked.shape[1]
    both = jnp.concatenate(split(values), axis=0)
    place = lax.broadcasted_iota(jnp.int32, (rows, devices), 0)
    for k in range(PAIRS):
        chosen = jnp.concatenate(
            [one_hot(place == asked[2 * k : 2 * k + 1]), one_hot(place == asked[2 * k + 1 : 2 * k + 2])], axis=1
        )
        got = mm(both, chosen)
        got = got[:width] + got[width:]
        stacked = jnp.concatenate([got[:, :devices], got[:, devices:]], axis=0)
        message_ref[message_rows(k, devices), :] = stacked.T


def rows_from_messages(message_ref, asked, rows):
    devices = asked.shape[1]
    width = LANES // 2
    place = lax.broadcasted_iota(jnp.int32, (rows, devices), 0)
    totals = [jnp.zeros((rows, 2 * LANES), F32), jnp.zeros((rows, 2 * LANES), F32)]
    for k in range(0, PAIRS, 2):
        parts = []
        for step in (k, k + 1):
            parts.append(jnp.concatenate(split(message_ref[message_rows(step, devices), :]), axis=1))
        parts = jnp.concatenate(parts, axis=0)
        for side in range(2):
            a, b = 2 * k + side, 2 * k + 2 + side
            chosen = jnp.concatenate(
                [one_hot(place == asked[a : a + 1]), one_hot(place == asked[b : b + 1])], axis=1
            )
            totals[side] = totals[side] + mm(chosen, parts)
    sides = [t[:, :LANES] + t[:, LANES:] for t in totals]
    lane = lax.broadcasted_iota(jnp.int32, (rows, LANES), 1)
    both = jnp.where(lane < width, sides[0], sides[1]).T
    return both[:width] + both[width:]


def fetch_kernel(request_ref, vector_ref, asked_ref, message_ref):
    asked = request_ref[...].astype(F32).T.astype(jnp.int32)[: 2 * PAIRS]
    asked_ref[...] = asked
    rows_to_messages(vector_ref[...], asked, message_ref)


def assemble_kernel(arrived_ref, asked_ref, message_ref, *, rows):
    asked = asked_ref[...]
    assembled = rows_from_messages(arrived_ref, asked, rows)
    rows_to_messages(assembled, asked, message_ref)


def two_sum(a, b):
    total = a + b
    back = total - a
    return total, (a - (total - back)) + (b - back)


def pair_add(a, b):
    total, rest = two_sum(a[0], b[0])
    return total, rest + (a[1] + b[1])


def store_sums(products, out_ref):
    row = lax.broadcasted_iota(jnp.int32, (8, LANES), 0)
    tiles = []
    for base in range(0, len(products), 8):
        tile = (jnp.zeros((8, LANES), F32), jnp.zeros((8, LANES), F32))
        for n, (left, right) in enumerate(products[base : base + 8]):
            width, rows = left.shape
            pair = (jnp.zeros((8, LANES), F32), jnp.zeros((8, LANES), F32))
            for a in range(0, width, 8):
                for b in range(0, rows, LANES):
                    term = left[a : a + 8, b : b + LANES] * right[a : a + 8, b : b + LANES]
                    total, rest = two_sum(pair[0], term)
                    pair = (total, pair[1] + rest)
            for shift in (4, 2, 1):
                pair = pair_add(pair, tuple(pltpu.roll(p, shift, 0) for p in pair))
            tile = tuple(jnp.where(row == n, p, t) for p, t in zip(pair, tile))
        shift = LANES // 2
        while shift:
            tile = pair_add(tile, tuple(pltpu.roll(t, shift, 1) for t in tile))
            shift //= 2
        tiles.append(tile)
    half = out_ref.shape[0] // 2
    for n, tile in enumerate(tiles):
        out_ref[n * 8 : (n + 1) * 8, :] = tile[0]
        out_ref[half + n * 8 : half + (n + 1) * 8, :] = tile[1]
    for n in range(len(tiles), half // 8):
        out_ref[n * 8 : (n + 1) * 8, :] = jnp.zeros((8, LANES), F32)
        out_ref[half + n * 8 : half + (n + 1) * 8, :] = jnp.zeros((8, LANES), F32)


def final_kernel(arrived_ref, asked_ref, basis_ref, gram_ref, image_ref, stats_ref, sums_ref):
    kb, width, rows = basis_ref.shape
    image = rows_from_messages(arrived_ref, asked_ref[...], rows)
    image_ref[...] = image
    store_sums([(image, image)] + [(image, basis_ref[k]) for k in range(kb)], sums_ref)
    used = sums_ref.shape[0] + gram_ref.shape[0]
    square = jnp.concatenate([sums_ref[...], gram_ref[...], jnp.zeros((LANES - used, LANES), F32)], axis=0)
    stats_ref[...] = square.T


def finish_kernel(gathered_ref, image_ref, basis_ref, direction_ref, coeff_ref, *, entries):
    kb = basis_ref.shape[0]
    devices = gathered_ref.shape[0]
    gram = 16
    high = gathered_ref[...]
    lane = lax.broadcasted_iota(jnp.int32, high.shape, 1)
    low = jnp.where(lane < gram, pltpu.roll(high, LANES - 8, 1), pltpu.roll(high, LANES - gram, 1))
    pair = (high, low)
    half = devices // 2
    pair = (high, low)
    while half >= 1:
        pair = pair_add(
            tuple(p[:half] for p in pair), tuple(p[half : 2 * half] for p in pair)
        )
        half //= 2
    lane = lax.broadcasted_iota(jnp.int32, (1, LANES), 1)

    def entry(n):
        return tuple(jnp.sum(jnp.where(lane == n, p, 0.0), axis=1, keepdims=True) for p in pair)

    numbers = [entry(n) for n in range(1 + kb)]
    numbers += [entry(gram + n) for n in range(kb * (kb + 1) // 2)]
    inv_root = 1.0 / math.sqrt(entries)
    projected = [(numbers[1 + k][0] + numbers[1 + k][1]) * inv_root for k in range(kb)]
    steps = [p * inv_root for p in projected]

    def add_product(total, factor, number):
        a, b = factor, number[0]
        a_high = a * 4097.0
        a_high = a_high - (a_high - a)
        b_high = b * 4097.0
        b_high = b_high - (b_high - b)
        a_low, b_low = a - a_high, b - b_high
        product = a * b
        rest = ((a_high * b_high - product) + a_high * b_low + a_low * b_high) + a_low * b_low
        return pair_add(total, (product, rest + factor * number[1]))

    def scaled(number, factor):
        zero = jnp.zeros_like(factor)
        return add_product((zero, zero), factor, number)

    total = numbers[0]
    at = 1 + kb
    for k in range(kb):
        total = add_product(total, -2.0 * steps[k], numbers[1 + k])
    for k in range(kb):
        for other in range(k, kb):
            factor = steps[k] if other == k else 2.0 * steps[k]
            total = add_product(total, factor, scaled(numbers[at], steps[other]))
            at += 1
    squares = jnp.maximum(total[0] + total[1], 0.0)
    root_mean = jnp.sqrt(squares / entries + 1e-06)
    remainder = image_ref[...]
    for k in range(kb):
        remainder = remainder - steps[k] * basis_ref[k]
    direction_ref[...] = remainder / root_mean
    coeffs = jnp.zeros((1, LANES), F32)
    for n, value in enumerate(projected + [root_mean]):
        coeffs = jnp.where(lane == n, value, coeffs)
    coeff_ref[...] = coeffs


def body(
    basis,
    interface_row_owner,
    interface_local_row,
    interface_slot_weight,
    local_inverse,
    prim_index,
    prim_vector,
    coarse_inverse,
    interface_shifted_diagonal,
    coupling_index,
    coupling_blocks,
    interior_inverse,
):
    span = lax.axis_size("span")
    devices = lax.axis_size("stream") * span
    kb, width, rows = basis.shape
    slots = interface_local_row.shape[0]
    kc, inner = coupling_index.shape
    nprim = prim_index.shape[0]
    entries = width * rows * devices
    owner = interface_row_owner.reshape(1, slots)
    row = interface_local_row.reshape(1, slots)
    weight = interface_slot_weight.reshape(1, slots)
    prim = prim_index.reshape(nprim, 1)
    shape = jax.ShapeDtypeStruct
    message = shape((devices * PAIRS, LANES), F32)
    field = shape((width, slots), F32)
    square = shape((devices, LANES), F32)

    def exchange(x, per):
        sent = x.reshape(devices, per, LANES)
        return lax.all_to_all(sent, ("stream", "span"), split_axis=0, concat_axis=0, tiled=True).reshape(x.shape)

    anywhere, here = pl.BlockSpec(memory_space=pltpu.HBM), pl.BlockSpec(memory_space=pltpu.VMEM)
    requests, ids = call(
        plan_kernel,
        (shape((devices, LANES), jnp.int32), shape((2, slots), jnp.int32)),
        owner,
        row,
        in_specs=[anywhere] * 2,
        scratch_shapes=[
            pltpu.VMEM((1, slots), jnp.int32),
            pltpu.VMEM((1, slots), jnp.int32),
            pltpu.SemaphoreType.DMA((2,)),
        ],
    )
    weight, chosen, vectors, coarse, named, gram, last = call(
        prepare_kernel,
        (
            shape((1, slots), F32),
            shape((nprim, slots), F32),
            shape((width, nprim), F32),
            shape((PAIRS * nprim, LANES), F32),
            shape((devices, nprim), BF16),
            shape((32, LANES), F32),
            shape((width, rows), F32),
        ),
        ids,
        weight,
        prim,
        prim_vector,
        basis,
    )
    arrived = exchange(requests, 1)
    asked, sent = call(
        fetch_kernel,
        (shape((2 * PAIRS, devices), jnp.int32), message),
        arrived,
        last,
    )
    restricted, contrib = call(
        restrict_kernel, (field, square), exchange(sent, PAIRS), ids, weight, chosen, vectors
    )
    contribs = exchange(contrib, 1)
    packed = call(
        neumann_kernel,
        message,
        local_inverse,
        restricted,
        ids,
        weight,
        vmem=50,
        in_specs=[anywhere, here, here, here],
        scratch_shapes=[
            pltpu.VMEM((width, slots), F32),
            pltpu.VMEM(local_inverse.shape, BF16),
            pltpu.SemaphoreType.DMA((slots // LANES,)),
        ],
    )
    sent = call(
        functools.partial(correct_kernel, span=span), message, packed, contribs, coarse_inverse, coarse, named
    )
    sent = call(functools.partial(assemble_kernel, rows=rows), message, exchange(sent, PAIRS), asked)
    sent = call(
        schur_kernel,
        message,
        exchange(sent, PAIRS),
        ids,
        coupling_index,
        interface_shifted_diagonal,
        coupling_blocks,
        interior_inverse,
        vmem=50,
        in_specs=[here] * 4 + [anywhere] * 2,
        scratch_shapes=[
            pltpu.VMEM((kc, width, inner), F32),
            pltpu.VMEM((width, inner), F32),
            pltpu.VMEM((kc, width, inner), F32),
            pltpu.VMEM(coupling_blocks.shape, BF16),
            pltpu.VMEM(interior_inverse.shape, BF16),
            pltpu.SemaphoreType.DMA((inner // LANES, 2)),
        ],
    )
    image, stats = call(
        final_kernel,
        (shape((width, rows), F32), square),
        exchange(sent, PAIRS),
        asked,
        basis,
        gram,
        scratch_shapes=[pltpu.VMEM((16, LANES), F32)],
    )
    direction, coeffs = call(
        functools.partial(finish_kernel, entries=entries),
        (shape((width, rows), F32), shape((1, LANES), F32)),
        exchange(stats, 1),
        image,
        basis,
    )
    return direction, coeffs[0, : kb + 1]


def solution(mesh):
    placed = (
        P(None, None, ("stream", "span")),
        P(("stream", "span"), None),
        P(("stream", "span")),
        P(("stream", "span")),
        P(None, None, ("stream", "span")),
        P(("stream", "span")),
        P(None, ("stream", "span")),
        P("stream", None),
        P(None, ("stream", "span")),
        P(None, ("stream", "span")),
        P(None, None, None, ("stream", "span")),
        P(None, None, ("stream", "span")),
    )
    return jax.shard_map(
        body,
        mesh=mesh,
        in_specs=placed,
        out_specs=(P(None, ("stream", "span")), P()),
        check_vma=False,
    )
```

```python
import functools
import math

import jax
import jax.numpy as jnp
from jax import lax
from jax.experimental import pallas as pl
from jax.experimental.pallas import tpu as pltpu
from jax.sharding import PartitionSpec as P

HIGH = lax.Precision.HIGHEST
F32 = jnp.float32
BF16 = jnp.bfloat16
LANES = 128
PAIRS = 8


def split(x):
    high = x.astype(BF16)
    return high, (x - high.astype(F32)).astype(BF16)


def mm(a, b):
    return jnp.dot(a, b, preferred_element_type=F32)


def mm_nt(a, b, precision=None):
    return lax.dot_general(a, b, (((1,), (1,)), ((), ())), precision=precision, preferred_element_type=F32)


def one_hot(mask):
    return jnp.where(mask, 1.0, 0.0).astype(BF16)


def message_rows(k, count):
    return pl.ds(k, count, stride=PAIRS)


def call(kernel, out_shape, *args, vmem=16, flops=0, **kw):
    if flops:
        kw["cost_estimate"] = pl.CostEstimate(flops=flops, bytes_accessed=flops // 100, transcendentals=0)
    return pl.pallas_call(
        kernel,
        out_shape=out_shape,
        compiler_params=pltpu.CompilerParams(vmem_limit_bytes=vmem * 1024 * 1024),
        **kw,
    )(*args)


def plan_kernel(row_of_ref, request_ref, ids_ref, *, rows):
    slots = row_of_ref.shape[1]
    devices = request_ref.shape[0]
    row_of = row_of_ref[...]
    owner = lax.div(row_of, rows)
    row = row_of - owner * rows
    named = one_hot(lax.broadcasted_iota(jnp.int32, (devices, slots), 0) == owner)
    before = lax.broadcasted_iota(jnp.int32, (LANES, LANES), 0) < lax.broadcasted_iota(
        jnp.int32, (LANES, LANES), 1
    )
    counter = jnp.concatenate([one_hot(before), jnp.ones((LANES, LANES), BF16)], axis=1)
    carry = jnp.zeros((devices, LANES), F32)
    ranks = []
    for block in range(slots // LANES):
        part = named[:, block * LANES : (block + 1) * LANES]
        counts = mm(part, counter)
        ranks.append(jnp.sum((counts[:, :LANES] + carry) * part.astype(F32), axis=0, keepdims=True))
        carry = carry + counts[:, LANES:]
    rank = jnp.concatenate(ranks, axis=1).astype(jnp.int32)
    ids_ref[0:1, :] = owner
    ids_ref[1:2, :] = rank
    at_rank = lax.broadcasted_iota(jnp.int32, (LANES, slots), 0) == rank
    tens = jnp.where(at_rank, (row >> 4).astype(F32), 0.0).astype(BF16)
    units = jnp.where(at_rank, (row & 15).astype(F32), 0.0).astype(BF16)
    request_ref[...] = (16.0 * mm_nt(named, tens) + mm_nt(named, units)).astype(jnp.int32)


def slots_from_messages(message_ref, owner, rank):
    slots = owner.shape[1]
    devices = message_ref.shape[0] // PAIRS
    width = LANES // 2
    sides = []
    for k in range(PAIRS):
        high, low = split(message_ref[message_rows(k, devices), :].T)
        sides.append(jnp.concatenate([high, low], axis=1))
    chunk = 256
    pieces = []
    for c in range(slots // chunk):
        lanes = slice(c * chunk, (c + 1) * chunk)
        named = one_hot(lax.broadcasted_iota(jnp.int32, (devices, chunk), 0) == owner[:, lanes])
        named = jnp.concatenate([named, named], axis=0)
        place = jnp.broadcast_to(rank[:, lanes], (width, chunk))
        total = jnp.zeros((width, chunk), F32)
        for k in range(PAIRS):
            both = mm(sides[k], named)
            total = jnp.where(place == 2 * k, both[:width], total)
            total = jnp.where(place == 2 * k + 1, both[width:], total)
        pieces.append(total)
    return jnp.concatenate(pieces, axis=1)


def slots_to_messages(values, owner, rank, message_ref):
    slots = owner.shape[1]
    devices = message_ref.shape[0] // PAIRS
    first = (rank & 1) == 0
    sides = jnp.concatenate([jnp.where(first, values, 0.0), jnp.where(first, 0.0, values)], axis=0).T
    sides = jnp.concatenate(split(sides), axis=1)
    named = one_hot(lax.broadcasted_iota(jnp.int32, (devices, slots), 0) == owner)
    pair = rank >> 1
    for k in range(PAIRS):
        both = mm(named * one_hot(pair == k), sides)
        message_ref[message_rows(k, devices), :] = both[:, :LANES] + both[:, LANES:]


def block_sums(block_refs, vectors, a, lanes):
    total = None
    for ref, vector in zip(block_refs, vectors):
        product = ref[a, :, lanes].astype(F32) * vector
        part = jnp.sum(product.reshape(product.shape[0] // 8, 8, LANES), axis=0)
        total = part if total is None else total + part
    for shift in (4, 2, 1):
        total = total + pltpu.roll(total, shift, 0)
    return total


def row_tile(block_refs, vectors, first, lanes):
    row = lax.broadcasted_iota(jnp.int32, (8, LANES), 0)
    result = jnp.zeros((8, LANES), F32)
    for j in range(8):
        result = jnp.where(row == j, block_sums(block_refs, vectors, first + j, lanes), result)
    return result


def apply_blocks(block_refs, vector_refs, out_ref, c):
    lanes = slice(c * LANES, (c + 1) * LANES)
    vectors = [ref[:, lanes] for ref in vector_refs]

    def rows_of(tile, _):
        first = pl.multiple_of(tile * 8, 8)
        out_ref[pl.ds(first, 8), lanes] = row_tile(block_refs, vectors, first, lanes)
        return 0

    lax.fori_loop(0, out_ref.shape[0] // 8, rows_of, 0)


def as_column(row):
    return jnp.broadcast_to(row.astype(F32), (8, row.shape[1])).T[:, :1]


def prepare_kernel(
    ids_ref,
    weight_ref,
    prim_ref,
    vector_ref,
    basis_ref,
    weights_ref,
    chosen_ref,
    vectors_ref,
    coarse_ref,
    named_ref,
    gram_ref,
    last_ref,
):
    slots = ids_ref.shape[1]
    nprim = vector_ref.shape[0]
    devices = named_ref.shape[0]
    prim = as_column(prim_ref[...])[:nprim].astype(jnp.int32)
    chosen = lax.broadcasted_iota(jnp.int32, (nprim, slots), 1) == prim
    weights_ref[...] = weight_ref[...]
    chosen_ref[...] = one_hot(chosen)
    vectors_ref[...] = vector_ref[...]

    def column(values):
        return jnp.sum(jnp.where(chosen, values.astype(F32), 0.0), axis=1, keepdims=True)

    weight, rank, owner = column(weight_ref[...]), column(ids_ref[1:2, :]), column(ids_ref[0:1, :])
    named_ref[...] = one_hot(
        lax.broadcasted_iota(jnp.int32, (nprim, devices), 1).astype(F32) == owner
    ).astype(F32).T.astype(BF16)
    vectors = vector_ref[...] * weight
    for k in range(PAIRS):
        sides = [jnp.where(rank == 2.0 * k + side, vectors, 0.0) for side in range(2)]
        coarse_ref[k * nprim : (k + 1) * nprim, :] = jnp.concatenate(sides, axis=1)
    kb = basis_ref.shape[0]
    fields = [basis_ref[k] for k in range(kb)]
    last_ref[...] = fields[kb - 1]
    store_sums([(fields[i], fields[j]) for i in range(kb) for j in range(i, kb)], gram_ref)


def restrict_kernel(
    message_ref, ids_ref, weight_ref, chosen_ref, vector_ref, out_ref, contrib_ref
):
    restricted = slots_from_messages(message_ref, ids_ref[0:1, :], ids_ref[1:2, :]) * weight_ref[...]
    out_ref[...] = restricted
    nprim = chosen_ref.shape[0]
    at_prim = sum(mm_nt(chosen_ref[...], part) for part in split(restricted))
    contrib = jnp.sum(at_prim * vector_ref[...], axis=1, keepdims=True)
    square = jnp.broadcast_to(contrib, (nprim, contrib_ref.shape[0])).T
    contrib_ref[...] = jnp.concatenate([square, jnp.zeros((square.shape[0], LANES - nprim), F32)], axis=1)


def neumann_kernel(blocks_hbm, restricted_ref, ids_ref, weight_ref, message_ref, piece_ref, blocks_ref, sems):
    width, slots = piece_ref.shape
    copies = []
    for n in range(width // 8):
        rows = pl.ds(n * 8, 8)
        copies.append(pltpu.make_async_copy(blocks_hbm.at[rows], blocks_ref.at[rows], sems.at[n]))
    for copy in copies:
        copy.start()
    for n, copy in enumerate(copies):
        copy.wait()

        def chunk(c, _, first=n * 8):
            lanes = pl.ds(pl.multiple_of(c * LANES, LANES), LANES)
            piece_ref[first : first + 8, lanes] = row_tile([blocks_ref], [restricted_ref[:, lanes]], first, lanes)
            return 0

        lax.fori_loop(0, slots // LANES, chunk, 0)
    slots_to_messages(piece_ref[...] * weight_ref[...], ids_ref[0:1, :], ids_ref[1:2, :], message_ref)


def correct_kernel(packed_ref, gathered_ref, inverse_ref, coarse_ref, named_ref, message_ref, *, span):
    devices, nprim = named_ref.shape
    ncs = inverse_ref.shape[1]
    contrib = gathered_ref[...][:, :nprim]
    lane = lax.broadcasted_iota(jnp.int32, (nprim, ncs), 1)
    spread = jnp.where(lax.rem(lane, nprim) == lax.broadcasted_iota(jnp.int32, (nprim, ncs), 0), 1.0, 0.0)
    tiled = jnp.dot(contrib, spread, precision=HIGH, preferred_element_type=F32)
    device = lax.broadcasted_iota(jnp.int32, (devices, ncs), 0)
    stream = lax.broadcasted_iota(jnp.int32, (devices, ncs), 1)
    mine = lax.div(device, span) == lax.div(stream, nprim)
    coarse_rhs = jnp.sum(jnp.where(mine, tiled, 0.0), axis=0, keepdims=True)
    coarse_sol = jnp.sum(inverse_ref[...] * coarse_rhs, axis=1, keepdims=True)
    for k in range(PAIRS):
        high, low = split(coarse_ref[k * nprim : (k + 1) * nprim, :] * coarse_sol)
        both = mm(named_ref[...], jnp.concatenate([high, low], axis=1))
        at = message_rows(k, devices)
        message_ref[at, :] = packed_ref[at, :] + (both[:, :LANES] + both[:, LANES:])


def schur_kernel(
    arrived_ref,
    ids_ref,
    index_ref,
    diagonal_ref,
    coupling_ref,
    inverse_ref,
    message_ref,
    gathered_ref,
    inner_ref,
    backward_ref,
):
    kc, inner = index_ref.shape
    chunks = inner // LANES
    owner, rank = ids_ref[0:1, :], ids_ref[1:2, :]
    restored = slots_from_messages(arrived_ref, owner, rank)
    width, slots = restored.shape
    both = jnp.concatenate(split(restored), axis=0)
    for k in range(kc):
        chosen = one_hot(lax.broadcasted_iota(jnp.int32, (slots, inner), 0) == index_ref[k : k + 1, :])
        got = mm(both, chosen)
        gathered_ref[k] = got[:width] + got[width:]
    blocks = [coupling_ref.at[k] for k in range(kc)]
    for c in range(chunks):
        apply_blocks(blocks, [gathered_ref.at[k] for k in range(kc)], inner_ref, c)
        lanes = slice(c * LANES, (c + 1) * LANES)
        vector = inner_ref[:, lanes]

        def step(tile, totals, lanes=lanes, vector=vector):
            for j in range(8):
                a = tile * 8 + j
                solved = block_sums([inverse_ref], [vector], a, lanes)
                totals = tuple(
                    total + ref[a, :, lanes].astype(F32).reshape(width // 8, 8, LANES) * solved[None]
                    for total, ref in zip(totals, blocks)
                )
            return totals

        zero = jnp.zeros((width // 8, 8, LANES), F32)
        totals = lax.fori_loop(0, width // 8, step, (zero,) * kc)
        for k in range(kc):
            backward_ref[k, :, lanes] = totals[k].reshape(width, LANES)
    value = diagonal_ref[...] * restored
    for k in range(kc):
        both = jnp.concatenate(split(backward_ref[k]), axis=0)
        index = as_column(index_ref[k : k + 1, :]).astype(jnp.int32)
        chosen = one_hot(lax.broadcasted_iota(jnp.int32, (inner, slots), 1) == index)
        got = mm(both, chosen)
        value = value - (got[:width] + got[width:])
    slots_to_messages(value, owner, rank, message_ref)


def rows_to_messages(values, asked, message_ref):
    width, rows = values.shape
    devices = asked.shape[1]
    both = jnp.concatenate(split(values), axis=0)
    place = lax.broadcasted_iota(jnp.int32, (rows, devices), 0)
    for k in range(PAIRS):
        chosen = jnp.concatenate(
            [one_hot(place == asked[2 * k : 2 * k + 1]), one_hot(place == asked[2 * k + 1 : 2 * k + 2])], axis=1
        )
        got = mm(both, chosen)
        got = got[:width] + got[width:]
        stacked = jnp.concatenate([got[:, :devices], got[:, devices:]], axis=0)
        message_ref[message_rows(k, devices), :] = stacked.T


def rows_from_messages(message_ref, asked, rows):
    devices = asked.shape[1]
    width = LANES // 2
    place = lax.broadcasted_iota(jnp.int32, (rows, devices), 0)
    totals = [jnp.zeros((rows, 2 * LANES), F32), jnp.zeros((rows, 2 * LANES), F32)]
    for k in range(0, PAIRS, 2):
        parts = []
        for step in (k, k + 1):
            parts.append(jnp.concatenate(split(message_ref[message_rows(step, devices), :]), axis=1))
        parts = jnp.concatenate(parts, axis=0)
        for side in range(2):
            a, b = 2 * k + side, 2 * k + 2 + side
            chosen = jnp.concatenate(
                [one_hot(place == asked[a : a + 1]), one_hot(place == asked[b : b + 1])], axis=1
            )
            totals[side] = totals[side] + mm(chosen, parts)
    sides = [t[:, :LANES] + t[:, LANES:] for t in totals]
    lane = lax.broadcasted_iota(jnp.int32, (rows, LANES), 1)
    both = jnp.where(lane < width, sides[0], sides[1]).T
    return both[:width] + both[width:]


def fetch_kernel(request_ref, vector_ref, asked_ref, message_ref):
    asked = request_ref[...].astype(F32).T.astype(jnp.int32)[: 2 * PAIRS]
    asked_ref[...] = asked
    rows_to_messages(vector_ref[...], asked, message_ref)


def assemble_kernel(arrived_ref, asked_ref, message_ref, *, rows):
    asked = asked_ref[...]
    assembled = rows_from_messages(arrived_ref, asked, rows)
    rows_to_messages(assembled, asked, message_ref)


def two_sum(a, b):
    total = a + b
    back = total - a
    return total, (a - (total - back)) + (b - back)


def pair_add(a, b):
    total, rest = two_sum(a[0], b[0])
    return total, rest + (a[1] + b[1])


def two_product(a, b):
    a_high = a * 4097.0
    a_high = a_high - (a_high - a)
    b_high = b * 4097.0
    b_high = b_high - (b_high - b)
    a_low, b_low = a - a_high, b - b_high
    product = a * b
    return product, ((a_high * b_high - product) + a_high * b_low + a_low * b_high) + a_low * b_low


def store_sums(products, out_ref):
    row = lax.broadcasted_iota(jnp.int32, (8, LANES), 0)
    tiles = []
    for base in range(0, len(products), 8):
        tile = (jnp.zeros((8, LANES), F32), jnp.zeros((8, LANES), F32))
        for n, (left, right) in enumerate(products[base : base + 8]):
            width, rows = left.shape
            pair = (jnp.zeros((8, LANES), F32), jnp.zeros((8, LANES), F32))
            for a in range(0, width, 8):
                for b in range(0, rows, LANES):
                    term = left[a : a + 8, b : b + LANES] * right[a : a + 8, b : b + LANES]
                    total, rest = two_sum(pair[0], term)
                    pair = (total, pair[1] + rest)
            for shift in (4, 2, 1):
                pair = pair_add(pair, tuple(pltpu.roll(p, shift, 0) for p in pair))
            tile = tuple(jnp.where(row == n, p, t) for p, t in zip(pair, tile))
        shift = LANES // 2
        while shift:
            tile = pair_add(tile, tuple(pltpu.roll(t, shift, 1) for t in tile))
            shift //= 2
        tiles.append(tile)
    half = out_ref.shape[0] // 2
    for n, tile in enumerate(tiles):
        out_ref[n * 8 : (n + 1) * 8, :] = tile[0]
        out_ref[half + n * 8 : half + (n + 1) * 8, :] = tile[1]
    for n in range(len(tiles), half // 8):
        out_ref[n * 8 : (n + 1) * 8, :] = jnp.zeros((8, LANES), F32)
        out_ref[half + n * 8 : half + (n + 1) * 8, :] = jnp.zeros((8, LANES), F32)


def final_kernel(arrived_ref, asked_ref, basis_ref, gram_ref, image_ref, stats_ref, sums_ref):
    kb, width, rows = basis_ref.shape
    image = rows_from_messages(arrived_ref, asked_ref[...], rows)
    image_ref[...] = image
    store_sums([(image, image)] + [(image, basis_ref[k]) for k in range(kb)], sums_ref)
    used = sums_ref.shape[0] + gram_ref.shape[0]
    square = jnp.concatenate([sums_ref[...], gram_ref[...], jnp.zeros((LANES - used, LANES), F32)], axis=0)
    stats_ref[...] = square.T


def finish_kernel(gathered_ref, image_ref, basis_ref, direction_ref, coeff_ref, *, entries):
    kb = basis_ref.shape[0]
    devices = gathered_ref.shape[0]
    gram = 16
    high = gathered_ref[...]
    lane = lax.broadcasted_iota(jnp.int32, high.shape, 1)
    low = jnp.where(lane < gram, pltpu.roll(high, LANES - 8, 1), pltpu.roll(high, LANES - gram, 1))
    pair = (high, low)
    half = devices // 2
    pair = (high, low)
    while half >= 1:
        pair = pair_add(
            tuple(p[:half] for p in pair), tuple(p[half : 2 * half] for p in pair)
        )
        half //= 2
    lane = lax.broadcasted_iota(jnp.int32, (1, LANES), 1)
    inv_root = 1.0 / math.sqrt(entries)
    projected = (pair[0] + pair[1]) * inv_root
    steps = [
        jnp.sum(jnp.where(lane == 1 + k, projected, 0.0), axis=1, keepdims=True) * inv_root for k in range(kb)
    ]
    left = jnp.where(lane == 0, 1.0, 0.0)
    right = jnp.ones((1, LANES), F32)
    at = gram
    for k in range(kb):
        left = jnp.where(lane == 1 + k, -2.0 * steps[k], left)
        for other in range(k, kb):
            left = jnp.where(lane == at, steps[k] if other == k else 2.0 * steps[k], left)
            right = jnp.where(lane == at, steps[other], right)
            at += 1
    factor, factor_rest = two_product(left, right)
    total, rest = two_product(factor, pair[0])
    pair = (total, rest + (factor * pair[1] + factor_rest * pair[0]))
    shift = gram
    while shift:
        pair = pair_add(pair, tuple(pltpu.roll(p, LANES - shift, 1) for p in pair))
        shift //= 2
    squares = jnp.maximum((pair[0] + pair[1])[:, :1], 0.0)
    root_mean = jnp.sqrt(squares / entries + 1e-06)
    remainder = image_ref[...]
    for k in range(kb):
        remainder = remainder - steps[k] * basis_ref[k]
    direction_ref[...] = remainder / root_mean
    values = jnp.where(lane == kb, root_mean, pltpu.roll(projected, LANES - 1, 1))
    coeff_ref[...] = values[0, : kb + 1]


def body(
    basis,
    interface_row_owner,
    interface_local_row,
    interface_slot_weight,
    local_inverse,
    prim_index,
    prim_vector,
    coarse_inverse,
    interface_shifted_diagonal,
    coupling_index,
    coupling_blocks,
    interior_inverse,
):
    span = lax.axis_size("span")
    devices = lax.axis_size("stream") * span
    kb, width, rows = basis.shape
    slots = interface_local_row.shape[0]
    kc, inner = coupling_index.shape
    nprim = prim_index.shape[0]
    entries = width * rows * devices
    owner = interface_row_owner.reshape(1, slots)
    row = interface_local_row.reshape(1, slots)
    weight = interface_slot_weight.reshape(1, slots)
    prim = prim_index.reshape(1, nprim)
    shape = jax.ShapeDtypeStruct
    message = shape((devices * PAIRS, LANES), F32)
    field = shape((width, slots), F32)
    square = shape((devices, LANES), F32)

    def exchange(x, per):
        sent = x.reshape(devices, per, LANES)
        return lax.all_to_all(sent, ("stream", "span"), split_axis=0, concat_axis=0, tiled=True).reshape(x.shape)

    requests, ids = call(
        functools.partial(plan_kernel, rows=rows),
        (shape((devices, LANES), jnp.int32), shape((2, slots), jnp.int32)),
        owner * rows + row,
        flops=20_000_000_000,
    )
    weight, chosen, vectors, coarse, named, gram, last = call(
        prepare_kernel,
        (
            shape((1, slots), F32),
            shape((nprim, slots), BF16),
            shape((nprim, width), F32),
            shape((PAIRS * nprim, LANES), F32),
            shape((devices, nprim), BF16),
            shape((32, LANES), F32),
            shape((width, rows), F32),
        ),
        ids,
        weight,
        prim,
        prim_vector.T,
        basis,
    )
    arrived = exchange(requests, 1)
    asked, sent = call(fetch_kernel, (shape((2 * PAIRS, devices), jnp.int32), message), arrived, last)
    anywhere, here = pl.BlockSpec(memory_space=pl.ANY), pl.BlockSpec(memory_space=pltpu.VMEM)
    restricted, contrib = call(
        restrict_kernel, (field, square), exchange(sent, PAIRS), ids, weight, chosen, vectors
    )
    contribs = exchange(contrib, 1)
    packed = call(
        neumann_kernel,
        message,
        local_inverse,
        restricted,
        ids,
        weight,
        vmem=50,
        in_specs=[anywhere, here, here, here],
        scratch_shapes=[
            pltpu.VMEM((width, slots), F32),
            pltpu.VMEM(local_inverse.shape, BF16),
            pltpu.SemaphoreType.DMA((width // 8,)),
        ],
    )
    sent = call(
        functools.partial(correct_kernel, span=span), message, packed, contribs, coarse_inverse, coarse, named
    )
    sent = call(
        functools.partial(assemble_kernel, rows=rows),
        message,
        exchange(sent, PAIRS),
        asked,
        flops=20_000_000_000,
    )
    sent = call(
        schur_kernel,
        message,
        exchange(sent, PAIRS),
        ids,
        coupling_index,
        interface_shifted_diagonal,
        coupling_blocks,
        interior_inverse,
        scratch_shapes=[
            pltpu.VMEM((kc, width, inner), F32),
            pltpu.VMEM((width, inner), F32),
            pltpu.VMEM((kc, width, inner), F32),
        ],
    )
    image, stats = call(
        final_kernel,
        (shape((width, rows), F32), square),
        exchange(sent, PAIRS),
        asked,
        basis,
        gram,
        scratch_shapes=[pltpu.VMEM((16, LANES), F32)],
    )
    return call(
        functools.partial(finish_kernel, entries=entries),
        (shape((width, rows), F32), shape((kb + 1,), F32)),
        exchange(stats, 1),
        image,
        basis,
    )


def solution(mesh):
    placed = (
        P(None, None, ("stream", "span")),
        P(("stream", "span"), None),
        P(("stream", "span")),
        P(("stream", "span")),
        P(None, None, ("stream", "span")),
        P(("stream", "span")),
        P(None, ("stream", "span")),
        P("stream", None),
        P(None, ("stream", "span")),
        P(None, ("stream", "span")),
        P(None, None, None, ("stream", "span")),
        P(None, None, ("stream", "span")),
    )
    return jax.shard_map(
        body,
        mesh=mesh,
        in_specs=placed,
        out_specs=(P(None, ("stream", "span")), P()),
        check_vma=False,
    )
```

```python
import functools
import math

import jax
import jax.numpy as jnp
from jax import lax
from jax.experimental import pallas as pl
from jax.experimental.pallas import tpu as pltpu
from jax.sharding import PartitionSpec as P

HIGH = lax.Precision.HIGHEST
F32 = jnp.float32
BF16 = jnp.bfloat16
LANES = 128
PAIRS = 8


def split(x):
    high = x.astype(BF16)
    return high, (x - high.astype(F32)).astype(BF16)


def mm(a, b):
    return jnp.dot(a, b, preferred_element_type=F32)


def mm_nt(a, b, precision=None):
    return lax.dot_general(a, b, (((1,), (1,)), ((), ())), precision=precision, preferred_element_type=F32)


def one_hot(mask):
    return jnp.where(mask, 1.0, 0.0).astype(BF16)


def message_rows(k, count):
    return pl.ds(k, count, stride=PAIRS)


def call(kernel, out_shape, *args, vmem=16, flops=0, **kw):
    if flops:
        kw["cost_estimate"] = pl.CostEstimate(flops=flops, bytes_accessed=flops // 100, transcendentals=0)
    return pl.pallas_call(
        kernel,
        out_shape=out_shape,
        compiler_params=pltpu.CompilerParams(vmem_limit_bytes=vmem * 1024 * 1024),
        **kw,
    )(*args)


def plan_kernel(owner_hbm, row_hbm, request_ref, ids_ref, owner_ref, row_ref, sems):
    slots = owner_ref.shape[1]
    devices = request_ref.shape[0]
    copies = [
        pltpu.make_async_copy(owner_hbm, owner_ref, sems.at[0]),
        pltpu.make_async_copy(row_hbm, row_ref, sems.at[1]),
    ]
    for copy in copies:
        copy.start()
    for copy in copies:
        copy.wait()
    owner = owner_ref[...]
    row = row_ref[...]
    named = one_hot(lax.broadcasted_iota(jnp.int32, (devices, slots), 0) == owner)
    before = lax.broadcasted_iota(jnp.int32, (LANES, LANES), 0) < lax.broadcasted_iota(
        jnp.int32, (LANES, LANES), 1
    )
    counter = jnp.concatenate([one_hot(before), jnp.ones((LANES, LANES), BF16)], axis=1)
    carry = jnp.zeros((devices, LANES), F32)
    ranks = []
    for block in range(slots // LANES):
        part = named[:, block * LANES : (block + 1) * LANES]
        counts = mm(part, counter)
        ranks.append(jnp.sum((counts[:, :LANES] + carry) * part.astype(F32), axis=0, keepdims=True))
        carry = carry + counts[:, LANES:]
    rank = jnp.concatenate(ranks, axis=1).astype(jnp.int32)
    ids_ref[0:1, :] = owner
    ids_ref[1:2, :] = rank
    at_rank = lax.broadcasted_iota(jnp.int32, (LANES, slots), 0) == rank
    tens = jnp.where(at_rank, (row >> 4).astype(F32), 0.0).astype(BF16)
    units = jnp.where(at_rank, (row & 15).astype(F32), 0.0).astype(BF16)
    request_ref[...] = (16.0 * mm_nt(named, tens) + mm_nt(named, units)).astype(jnp.int32)


def slots_from_messages(message_ref, owner, rank):
    slots = owner.shape[1]
    devices = message_ref.shape[0] // PAIRS
    width = LANES // 2
    sides = []
    for k in range(PAIRS):
        high, low = split(message_ref[message_rows(k, devices), :].T)
        sides.append(jnp.concatenate([high, low], axis=1))
    chunk = 256
    pieces = []
    for c in range(slots // chunk):
        lanes = slice(c * chunk, (c + 1) * chunk)
        named = one_hot(lax.broadcasted_iota(jnp.int32, (devices, chunk), 0) == owner[:, lanes])
        named = jnp.concatenate([named, named], axis=0)
        place = jnp.broadcast_to(rank[:, lanes], (width, chunk))
        total = jnp.zeros((width, chunk), F32)
        for k in range(PAIRS):
            both = mm(sides[k], named)
            total = jnp.where(place == 2 * k, both[:width], total)
            total = jnp.where(place == 2 * k + 1, both[width:], total)
        pieces.append(total)
    return jnp.concatenate(pieces, axis=1)


def slots_to_messages(values, owner, rank, message_ref):
    slots = owner.shape[1]
    devices = message_ref.shape[0] // PAIRS
    first = (rank & 1) == 0
    sides = jnp.concatenate([jnp.where(first, values, 0.0), jnp.where(first, 0.0, values)], axis=0).T
    sides = jnp.concatenate(split(sides), axis=1)
    named = one_hot(lax.broadcasted_iota(jnp.int32, (devices, slots), 0) == owner)
    pair = rank >> 1
    for k in range(PAIRS):
        both = mm(named * one_hot(pair == k), sides)
        message_ref[message_rows(k, devices), :] = both[:, :LANES] + both[:, LANES:]


def block_sums(block_refs, vectors, a, lanes):
    total = None
    for ref, vector in zip(block_refs, vectors):
        product = ref[a, :, lanes].astype(F32) * vector
        part = jnp.sum(product.reshape(product.shape[0] // 8, 8, LANES), axis=0)
        total = part if total is None else total + part
    for shift in (4, 2, 1):
        total = total + pltpu.roll(total, shift, 0)
    return total


def row_tile(block_refs, vectors, first, lanes):
    row = lax.broadcasted_iota(jnp.int32, (8, LANES), 0)
    result = jnp.zeros((8, LANES), F32)
    for j in range(8):
        result = jnp.where(row == j, block_sums(block_refs, vectors, first + j, lanes), result)
    return result


def apply_blocks(block_refs, vector_refs, out_ref, c):
    lanes = slice(c * LANES, (c + 1) * LANES)
    vectors = [ref[:, lanes] for ref in vector_refs]

    def rows_of(tile, _):
        first = pl.multiple_of(tile * 8, 8)
        out_ref[pl.ds(first, 8), lanes] = row_tile(block_refs, vectors, first, lanes)
        return 0

    lax.fori_loop(0, out_ref.shape[0] // 8, rows_of, 0)


def as_column(row):
    return jnp.broadcast_to(row.astype(F32), (8, row.shape[1])).T[:, :1]


def prepare_kernel(
    ids_ref,
    weight_ref,
    prim_ref,
    vector_ref,
    basis_ref,
    blocks_hbm,
    kept_ref,
    weights_ref,
    chosen_ref,
    vectors_ref,
    coarse_ref,
    named_ref,
    gram_ref,
    last_ref,
    early_ref,
    sem,
):
    early = pltpu.make_async_copy(blocks_hbm.at[: early_ref.shape[0]], early_ref, sem)
    early.start()
    slots = ids_ref.shape[1]
    nprim = vector_ref.shape[0]
    devices = named_ref.shape[0]
    prim = as_column(prim_ref[...])[:nprim].astype(jnp.int32)
    chosen = lax.broadcasted_iota(jnp.int32, (nprim, slots), 1) == prim
    kept_ref[...] = ids_ref[...]
    weights_ref[...] = weight_ref[...]
    chosen_ref[...] = one_hot(chosen)
    vectors_ref[...] = vector_ref[...]

    def column(values):
        return jnp.sum(jnp.where(chosen, values.astype(F32), 0.0), axis=1, keepdims=True)

    weight, rank, owner = column(weight_ref[...]), column(ids_ref[1:2, :]), column(ids_ref[0:1, :])
    named_ref[...] = one_hot(
        lax.broadcasted_iota(jnp.int32, (nprim, devices), 1).astype(F32) == owner
    ).astype(F32).T.astype(BF16)
    vectors = vector_ref[...] * weight
    for k in range(PAIRS):
        sides = [jnp.where(rank == 2.0 * k + side, vectors, 0.0) for side in range(2)]
        coarse_ref[k * nprim : (k + 1) * nprim, :] = jnp.concatenate(sides, axis=1)
    kb = basis_ref.shape[0]
    fields = [basis_ref[k] for k in range(kb)]
    last_ref[...] = fields[kb - 1]
    store_sums([(fields[i], fields[j]) for i in range(kb) for j in range(i, kb)], gram_ref)
    early.wait()


def restrict_kernel(
    message_ref, ids_ref, weight_ref, chosen_ref, vector_ref, out_ref, contrib_ref
):
    restricted = slots_from_messages(message_ref, ids_ref[0:1, :], ids_ref[1:2, :]) * weight_ref[...]
    out_ref[...] = restricted
    nprim = chosen_ref.shape[0]
    at_prim = sum(mm_nt(chosen_ref[...], part) for part in split(restricted))
    contrib = jnp.sum(at_prim * vector_ref[...], axis=1, keepdims=True)
    square = jnp.broadcast_to(contrib, (nprim, contrib_ref.shape[0])).T
    contrib_ref[...] = jnp.concatenate([square, jnp.zeros((square.shape[0], LANES - nprim), F32)], axis=1)


def neumann_kernel(
    early_ref, blocks_hbm, restricted_ref, ids_ref, weight_ref, message_ref, piece_ref, blocks_ref, sems
):
    width, slots = piece_ref.shape
    held = early_ref.shape[0]
    copies = []
    for n, first in enumerate(range(held, width, 8)):
        copies.append(
            pltpu.make_async_copy(
                blocks_hbm.at[first : first + 8], blocks_ref.at[first - held : first - held + 8], sems.at[n]
            )
        )
    for copy in copies:
        copy.start()
    for first in range(0, width, 8):
        ref, start = early_ref, first
        if first >= held:
            copies[(first - held) // 8].wait()
            ref, start = blocks_ref, first - held

        def chunk(c, _, ref=ref, start=start, first=first):
            lanes = pl.ds(pl.multiple_of(c * LANES, LANES), LANES)
            piece_ref[first : first + 8, lanes] = row_tile([ref], [restricted_ref[:, lanes]], start, lanes)
            return 0

        lax.fori_loop(0, slots // LANES, chunk, 0)
    slots_to_messages(piece_ref[...] * weight_ref[...], ids_ref[0:1, :], ids_ref[1:2, :], message_ref)


def correct_kernel(packed_ref, gathered_ref, inverse_ref, coarse_ref, named_ref, message_ref, *, span):
    devices, nprim = named_ref.shape
    ncs = inverse_ref.shape[1]
    contrib = gathered_ref[...][:, :nprim]
    lane = lax.broadcasted_iota(jnp.int32, (nprim, ncs), 1)
    spread = jnp.where(lax.rem(lane, nprim) == lax.broadcasted_iota(jnp.int32, (nprim, ncs), 0), 1.0, 0.0)
    tiled = jnp.dot(contrib, spread, precision=HIGH, preferred_element_type=F32)
    device = lax.broadcasted_iota(jnp.int32, (devices, ncs), 0)
    stream = lax.broadcasted_iota(jnp.int32, (devices, ncs), 1)
    mine = lax.div(device, span) == lax.div(stream, nprim)
    coarse_rhs = jnp.sum(jnp.where(mine, tiled, 0.0), axis=0, keepdims=True)
    coarse_sol = jnp.sum(inverse_ref[...] * coarse_rhs, axis=1, keepdims=True)
    for k in range(PAIRS):
        high, low = split(coarse_ref[k * nprim : (k + 1) * nprim, :] * coarse_sol)
        both = mm(named_ref[...], jnp.concatenate([high, low], axis=1))
        at = message_rows(k, devices)
        message_ref[at, :] = packed_ref[at, :] + (both[:, :LANES] + both[:, LANES:])


def schur_kernel(
    arrived_ref,
    ids_ref,
    index_ref,
    diagonal_ref,
    coupling_ref,
    inverse_ref,
    message_ref,
    gathered_ref,
    inner_ref,
    backward_ref,
):
    kc, inner = index_ref.shape
    chunks = inner // LANES
    owner, rank = ids_ref[0:1, :], ids_ref[1:2, :]
    restored = slots_from_messages(arrived_ref, owner, rank)
    width, slots = restored.shape
    both = jnp.concatenate(split(restored), axis=0)
    for k in range(kc):
        chosen = one_hot(lax.broadcasted_iota(jnp.int32, (slots, inner), 0) == index_ref[k : k + 1, :])
        got = mm(both, chosen)
        gathered_ref[k] = got[:width] + got[width:]
    blocks = [coupling_ref.at[k] for k in range(kc)]
    for c in range(chunks):
        apply_blocks(blocks, [gathered_ref.at[k] for k in range(kc)], inner_ref, c)
        lanes = slice(c * LANES, (c + 1) * LANES)
        vector = inner_ref[:, lanes]

        def step(tile, totals, lanes=lanes, vector=vector):
            for j in range(8):
                a = tile * 8 + j
                solved = block_sums([inverse_ref], [vector], a, lanes)
                totals = tuple(
                    total + ref[a, :, lanes].astype(F32).reshape(width // 8, 8, LANES) * solved[None]
                    for total, ref in zip(totals, blocks)
                )
            return totals

        zero = jnp.zeros((width // 8, 8, LANES), F32)
        totals = lax.fori_loop(0, width // 8, step, (zero,) * kc)
        for k in range(kc):
            backward_ref[k, :, lanes] = totals[k].reshape(width, LANES)
    value = diagonal_ref[...] * restored
    for k in range(kc):
        both = jnp.concatenate(split(backward_ref[k]), axis=0)
        index = as_column(index_ref[k : k + 1, :]).astype(jnp.int32)
        chosen = one_hot(lax.broadcasted_iota(jnp.int32, (inner, slots), 1) == index)
        got = mm(both, chosen)
        value = value - (got[:width] + got[width:])
    slots_to_messages(value, owner, rank, message_ref)


def rows_to_messages(values, asked, message_ref):
    width, rows = values.shape
    devices = asked.shape[1]
    both = jnp.concatenate(split(values), axis=0)
    place = lax.broadcasted_iota(jnp.int32, (rows, devices), 0)
    for k in range(PAIRS):
        chosen = jnp.concatenate(
            [one_hot(place == asked[2 * k : 2 * k + 1]), one_hot(place == asked[2 * k + 1 : 2 * k + 2])], axis=1
        )
        got = mm(both, chosen)
        got = got[:width] + got[width:]
        stacked = jnp.concatenate([got[:, :devices], got[:, devices:]], axis=0)
        message_ref[message_rows(k, devices), :] = stacked.T


def rows_from_messages(message_ref, asked, rows):
    devices = asked.shape[1]
    width = LANES // 2
    place = lax.broadcasted_iota(jnp.int32, (rows, devices), 0)
    totals = [jnp.zeros((rows, 2 * LANES), F32), jnp.zeros((rows, 2 * LANES), F32)]
    for k in range(0, PAIRS, 2):
        parts = []
        for step in (k, k + 1):
            parts.append(jnp.concatenate(split(message_ref[message_rows(step, devices), :]), axis=1))
        parts = jnp.concatenate(parts, axis=0)
        for side in range(2):
            a, b = 2 * k + side, 2 * k + 2 + side
            chosen = jnp.concatenate(
                [one_hot(place == asked[a : a + 1]), one_hot(place == asked[b : b + 1])], axis=1
            )
            totals[side] = totals[side] + mm(chosen, parts)
    sides = [t[:, :LANES] + t[:, LANES:] for t in totals]
    lane = lax.broadcasted_iota(jnp.int32, (rows, LANES), 1)
    both = jnp.where(lane < width, sides[0], sides[1]).T
    return both[:width] + both[width:]


def fetch_kernel(request_ref, vector_ref, asked_ref, message_ref):
    asked = request_ref[...].astype(F32).T.astype(jnp.int32)[: 2 * PAIRS]
    asked_ref[...] = asked
    rows_to_messages(vector_ref[...], asked, message_ref)


def assemble_kernel(arrived_ref, asked_ref, message_ref, *, rows):
    asked = asked_ref[...]
    assembled = rows_from_messages(arrived_ref, asked, rows)
    rows_to_messages(assembled, asked, message_ref)


def two_sum(a, b):
    total = a + b
    back = total - a
    return total, (a - (total - back)) + (b - back)


def pair_add(a, b):
    total, rest = two_sum(a[0], b[0])
    return total, rest + (a[1] + b[1])


def two_product(a, b):
    a_high = a * 4097.0
    a_high = a_high - (a_high - a)
    b_high = b * 4097.0
    b_high = b_high - (b_high - b)
    a_low, b_low = a - a_high, b - b_high
    product = a * b
    return product, ((a_high * b_high - product) + a_high * b_low + a_low * b_high) + a_low * b_low


def store_sums(products, out_ref):
    row = lax.broadcasted_iota(jnp.int32, (8, LANES), 0)
    tiles = []
    for base in range(0, len(products), 8):
        tile = (jnp.zeros((8, LANES), F32), jnp.zeros((8, LANES), F32))
        for n, (left, right) in enumerate(products[base : base + 8]):
            width, rows = left.shape
            pair = (jnp.zeros((8, LANES), F32), jnp.zeros((8, LANES), F32))
            for a in range(0, width, 8):
                for b in range(0, rows, LANES):
                    term = left[a : a + 8, b : b + LANES] * right[a : a + 8, b : b + LANES]
                    total, rest = two_sum(pair[0], term)
                    pair = (total, pair[1] + rest)
            for shift in (4, 2, 1):
                pair = pair_add(pair, tuple(pltpu.roll(p, shift, 0) for p in pair))
            tile = tuple(jnp.where(row == n, p, t) for p, t in zip(pair, tile))
        shift = LANES // 2
        while shift:
            tile = pair_add(tile, tuple(pltpu.roll(t, shift, 1) for t in tile))
            shift //= 2
        tiles.append(tile)
    half = out_ref.shape[0] // 2
    for n, tile in enumerate(tiles):
        out_ref[n * 8 : (n + 1) * 8, :] = tile[0]
        out_ref[half + n * 8 : half + (n + 1) * 8, :] = tile[1]
    for n in range(len(tiles), half // 8):
        out_ref[n * 8 : (n + 1) * 8, :] = jnp.zeros((8, LANES), F32)
        out_ref[half + n * 8 : half + (n + 1) * 8, :] = jnp.zeros((8, LANES), F32)


def final_kernel(arrived_ref, asked_ref, basis_ref, gram_ref, image_ref, stats_ref, sums_ref):
    kb, width, rows = basis_ref.shape
    image = rows_from_messages(arrived_ref, asked_ref[...], rows)
    image_ref[...] = image
    store_sums([(image, image)] + [(image, basis_ref[k]) for k in range(kb)], sums_ref)
    used = sums_ref.shape[0] + gram_ref.shape[0]
    square = jnp.concatenate([sums_ref[...], gram_ref[...], jnp.zeros((LANES - used, LANES), F32)], axis=0)
    stats_ref[...] = square.T


def finish_kernel(gathered_ref, image_ref, basis_ref, direction_ref, coeff_ref, *, entries):
    kb = basis_ref.shape[0]
    devices = gathered_ref.shape[0]
    gram = 16
    high = gathered_ref[...]
    lane = lax.broadcasted_iota(jnp.int32, high.shape, 1)
    low = jnp.where(lane < gram, pltpu.roll(high, LANES - 8, 1), pltpu.roll(high, LANES - gram, 1))
    pair = (high, low)
    half = devices // 2
    pair = (high, low)
    while half >= 1:
        pair = pair_add(
            tuple(p[:half] for p in pair), tuple(p[half : 2 * half] for p in pair)
        )
        half //= 2
    lane = lax.broadcasted_iota(jnp.int32, (1, LANES), 1)
    inv_root = 1.0 / math.sqrt(entries)
    projected = (pair[0] + pair[1]) * inv_root
    steps = [
        jnp.sum(jnp.where(lane == 1 + k, projected, 0.0), axis=1, keepdims=True) * inv_root for k in range(kb)
    ]
    left = jnp.where(lane == 0, 1.0, 0.0)
    right = jnp.ones((1, LANES), F32)
    at = gram
    for k in range(kb):
        left = jnp.where(lane == 1 + k, -2.0 * steps[k], left)
        for other in range(k, kb):
            left = jnp.where(lane == at, steps[k] if other == k else 2.0 * steps[k], left)
            right = jnp.where(lane == at, steps[other], right)
            at += 1
    factor, factor_rest = two_product(left, right)
    total, rest = two_product(factor, pair[0])
    pair = (total, rest + (factor * pair[1] + factor_rest * pair[0]))
    shift = gram
    while shift:
        pair = pair_add(pair, tuple(pltpu.roll(p, LANES - shift, 1) for p in pair))
        shift //= 2
    squares = jnp.maximum((pair[0] + pair[1])[:, :1], 0.0)
    root_mean = jnp.sqrt(squares / entries + 1e-06)
    remainder = image_ref[...]
    for k in range(kb):
        remainder = remainder - steps[k] * basis_ref[k]
    direction_ref[...] = remainder / root_mean
    values = jnp.where(lane == kb, root_mean, pltpu.roll(projected, LANES - 1, 1))
    coeff_ref[...] = values[0, : kb + 1]


def body(
    basis,
    interface_row_owner,
    interface_local_row,
    interface_slot_weight,
    local_inverse,
    prim_index,
    prim_vector,
    coarse_inverse,
    interface_shifted_diagonal,
    coupling_index,
    coupling_blocks,
    interior_inverse,
):
    span = lax.axis_size("span")
    devices = lax.axis_size("stream") * span
    kb, width, rows = basis.shape
    slots = interface_local_row.shape[0]
    kc, inner = coupling_index.shape
    nprim = prim_index.shape[0]
    entries = width * rows * devices
    owner = interface_row_owner.reshape(1, slots)
    row = interface_local_row.reshape(1, slots)
    weight = interface_slot_weight.reshape(1, slots)
    prim = prim_index.reshape(1, nprim)
    shape = jax.ShapeDtypeStruct
    message = shape((devices * PAIRS, LANES), F32)
    field = shape((width, slots), F32)
    square = shape((devices, LANES), F32)

    def exchange(x, per):
        sent = x.reshape(devices, per, LANES)
        return lax.all_to_all(sent, ("stream", "span"), split_axis=0, concat_axis=0, tiled=True).reshape(x.shape)

    anywhere, here = pl.BlockSpec(memory_space=pl.ANY), pl.BlockSpec(memory_space=pltpu.VMEM)
    requests, ids = call(
        plan_kernel,
        (shape((devices, LANES), jnp.int32), shape((2, slots), jnp.int32)),
        owner,
        row,
        vmem=54,
        flops=20_000_000_000,
        in_specs=[anywhere] * 2,
        scratch_shapes=[
            pltpu.VMEM((1, slots), jnp.int32),
            pltpu.VMEM((1, slots), jnp.int32),
            pltpu.SemaphoreType.DMA((2,)),
        ],
    )
    held = 8
    ids, weight, chosen, vectors, coarse, named, gram, last, early = call(
        prepare_kernel,
        (
            shape((2, slots), jnp.int32),
            shape((1, slots), F32),
            shape((nprim, slots), BF16),
            shape((nprim, width), F32),
            shape((PAIRS * nprim, LANES), F32),
            shape((devices, nprim), BF16),
            shape((32, LANES), F32),
            shape((width, rows), F32),
            shape((held, width, slots), BF16),
        ),
        ids,
        weight,
        prim,
        prim_vector.T,
        basis,
        local_inverse,
        vmem=47,
        in_specs=[here] * 5 + [anywhere],
        scratch_shapes=[pltpu.SemaphoreType.DMA],
    )
    arrived = exchange(requests, 1)
    asked, sent = call(fetch_kernel, (shape((2 * PAIRS, devices), jnp.int32), message), arrived, last)
    restricted, contrib = call(
        restrict_kernel, (field, square), exchange(sent, PAIRS), ids, weight, chosen, vectors
    )
    contribs = exchange(contrib, 1)
    packed = call(
        neumann_kernel,
        message,
        early,
        local_inverse,
        restricted,
        ids,
        weight,
        vmem=50,
        in_specs=[here, anywhere, here, here, here],
        scratch_shapes=[
            pltpu.VMEM((width, slots), F32),
            pltpu.VMEM((width - held, width, slots), BF16),
            pltpu.SemaphoreType.DMA(((width - held) // 8,)),
        ],
    )
    sent = call(
        functools.partial(correct_kernel, span=span), message, packed, contribs, coarse_inverse, coarse, named
    )
    sent = call(
        functools.partial(assemble_kernel, rows=rows),
        message,
        exchange(sent, PAIRS),
        asked,
        flops=20_000_000_000,
    )
    sent = call(
        schur_kernel,
        message,
        exchange(sent, PAIRS),
        ids,
        coupling_index,
        interface_shifted_diagonal,
        coupling_blocks,
        interior_inverse,
        scratch_shapes=[
            pltpu.VMEM((kc, width, inner), F32),
            pltpu.VMEM((width, inner), F32),
            pltpu.VMEM((kc, width, inner), F32),
        ],
    )
    image, stats = call(
        final_kernel,
        (shape((width, rows), F32), square),
        exchange(sent, PAIRS),
        asked,
        basis,
        gram,
        scratch_shapes=[pltpu.VMEM((16, LANES), F32)],
    )
    return call(
        functools.partial(finish_kernel, entries=entries),
        (shape((width, rows), F32), shape((kb + 1,), F32)),
        exchange(stats, 1),
        image,
        basis,
    )


def solution(mesh):
    placed = (
        P(None, None, ("stream", "span")),
        P(("stream", "span"), None),
        P(("stream", "span")),
        P(("stream", "span")),
        P(None, None, ("stream", "span")),
        P(("stream", "span")),
        P(None, ("stream", "span")),
        P("stream", None),
        P(None, ("stream", "span")),
        P(None, ("stream", "span")),
        P(None, None, None, ("stream", "span")),
        P(None, None, ("stream", "span")),
    )
    return jax.shard_map(
        body,
        mesh=mesh,
        in_specs=placed,
        out_specs=(P(None, ("stream", "span")), P()),
        check_vma=False,
    )
```

```python
import functools
import math

import jax
import jax.numpy as jnp
from jax import lax
from jax.experimental import pallas as pl
from jax.experimental.pallas import tpu as pltpu
from jax.sharding import PartitionSpec as P

HIGH = lax.Precision.HIGHEST
F32 = jnp.float32
BF16 = jnp.bfloat16
LANES = 128
PAIRS = 8


def split(x):
    high = x.astype(BF16)
    return high, (x - high.astype(F32)).astype(BF16)


def mm(a, b):
    return jnp.dot(a, b, preferred_element_type=F32)


def mm_nt(a, b, precision=None):
    return lax.dot_general(a, b, (((1,), (1,)), ((), ())), precision=precision, preferred_element_type=F32)


def one_hot(mask):
    return jnp.where(mask, 1.0, 0.0).astype(BF16)


def message_rows(k, count):
    return pl.ds(k, count, stride=PAIRS)


def call(kernel, out_shape, *args, vmem=16, flops=0, **kw):
    if flops:
        kw["cost_estimate"] = pl.CostEstimate(flops=flops, bytes_accessed=flops // 100, transcendentals=0)
    return pl.pallas_call(
        kernel,
        out_shape=out_shape,
        compiler_params=pltpu.CompilerParams(vmem_limit_bytes=vmem * 1024 * 1024),
        **kw,
    )(*args)


def plan_kernel(owner_hbm, row_hbm, request_ref, ids_ref, owner_ref, row_ref, sems):
    slots = owner_ref.shape[1]
    devices = request_ref.shape[0]
    copies = [
        pltpu.make_async_copy(owner_hbm, owner_ref, sems.at[0]),
        pltpu.make_async_copy(row_hbm, row_ref, sems.at[1]),
    ]
    for copy in copies:
        copy.start()
    for copy in copies:
        copy.wait()
    owner = owner_ref[...]
    row = row_ref[...]
    named = one_hot(lax.broadcasted_iota(jnp.int32, (devices, slots), 0) == owner)
    before = lax.broadcasted_iota(jnp.int32, (LANES, LANES), 0) < lax.broadcasted_iota(
        jnp.int32, (LANES, LANES), 1
    )
    counter = jnp.concatenate([one_hot(before), jnp.ones((LANES, LANES), BF16)], axis=1)
    carry = jnp.zeros((devices, LANES), F32)
    ranks = []
    for block in range(slots // LANES):
        part = named[:, block * LANES : (block + 1) * LANES]
        counts = mm(part, counter)
        ranks.append(jnp.sum((counts[:, :LANES] + carry) * part.astype(F32), axis=0, keepdims=True))
        carry = carry + counts[:, LANES:]
    rank = jnp.concatenate(ranks, axis=1).astype(jnp.int32)
    ids_ref[0:1, :] = owner
    ids_ref[1:2, :] = rank
    at_rank = lax.broadcasted_iota(jnp.int32, (LANES, slots), 0) == rank
    tens = jnp.where(at_rank, (row >> 4).astype(F32), 0.0).astype(BF16)
    units = jnp.where(at_rank, (row & 15).astype(F32), 0.0).astype(BF16)
    request_ref[...] = (16.0 * mm_nt(named, tens) + mm_nt(named, units)).astype(jnp.int32)


def slots_from_messages(message_ref, owner, rank):
    slots = owner.shape[1]
    devices = message_ref.shape[0] // PAIRS
    width = LANES // 2
    sides = []
    for k in range(PAIRS):
        high, low = split(message_ref[message_rows(k, devices), :].T)
        sides.append(jnp.concatenate([high, low], axis=1))
    chunk = 256
    pieces = []
    for c in range(slots // chunk):
        lanes = slice(c * chunk, (c + 1) * chunk)
        named = one_hot(lax.broadcasted_iota(jnp.int32, (devices, chunk), 0) == owner[:, lanes])
        named = jnp.concatenate([named, named], axis=0)
        place = jnp.broadcast_to(rank[:, lanes], (width, chunk))
        total = jnp.zeros((width, chunk), F32)
        for k in range(PAIRS):
            both = mm(sides[k], named)
            total = jnp.where(place == 2 * k, both[:width], total)
            total = jnp.where(place == 2 * k + 1, both[width:], total)
        pieces.append(total)
    return jnp.concatenate(pieces, axis=1)


def slots_to_messages(values, owner, rank, message_ref):
    slots = owner.shape[1]
    devices = message_ref.shape[0] // PAIRS
    first = (rank & 1) == 0
    sides = jnp.concatenate([jnp.where(first, values, 0.0), jnp.where(first, 0.0, values)], axis=0).T
    sides = jnp.concatenate(split(sides), axis=1)
    named = one_hot(lax.broadcasted_iota(jnp.int32, (devices, slots), 0) == owner)
    pair = rank >> 1
    for k in range(PAIRS):
        both = mm(named * one_hot(pair == k), sides)
        message_ref[message_rows(k, devices), :] = both[:, :LANES] + both[:, LANES:]


def block_sums(block_refs, vectors, a, lanes):
    total = None
    for ref, vector in zip(block_refs, vectors):
        product = ref[a, :, lanes].astype(F32) * vector
        part = jnp.sum(product.reshape(product.shape[0] // 8, 8, LANES), axis=0)
        total = part if total is None else total + part
    for shift in (4, 2, 1):
        total = total + pltpu.roll(total, shift, 0)
    return total


def row_tile(block_refs, vectors, first, lanes):
    return tile_of([(block_refs, first + j) for j in range(8)], vectors, lanes)


def tile_of(places, vectors, lanes):
    row = lax.broadcasted_iota(jnp.int32, (8, LANES), 0)
    result = jnp.zeros((8, LANES), F32)
    for j, (refs, a) in enumerate(places):
        result = jnp.where(row == j, block_sums(refs, vectors, a, lanes), result)
    return result


def apply_blocks(block_refs, vector_refs, out_ref, c):
    lanes = slice(c * LANES, (c + 1) * LANES)
    vectors = [ref[:, lanes] for ref in vector_refs]

    def rows_of(tile, _):
        first = pl.multiple_of(tile * 8, 8)
        out_ref[pl.ds(first, 8), lanes] = row_tile(block_refs, vectors, first, lanes)
        return 0

    lax.fori_loop(0, out_ref.shape[0] // 8, rows_of, 0)


def as_column(row):
    return jnp.broadcast_to(row.astype(F32), (8, row.shape[1])).T[:, :1]


def prepare_kernel(
    ids_ref,
    weight_ref,
    prim_ref,
    vector_ref,
    basis_ref,
    blocks_hbm,
    kept_ref,
    weights_ref,
    chosen_ref,
    vectors_ref,
    coarse_ref,
    named_ref,
    gram_ref,
    last_ref,
    early_ref,
    sem,
):
    early = pltpu.make_async_copy(blocks_hbm.at[: early_ref.shape[0]], early_ref, sem)
    early.start()
    slots = ids_ref.shape[1]
    nprim = vector_ref.shape[0]
    devices = named_ref.shape[0]
    prim = as_column(prim_ref[...])[:nprim].astype(jnp.int32)
    chosen = lax.broadcasted_iota(jnp.int32, (nprim, slots), 1) == prim
    kept_ref[...] = ids_ref[...]
    weights_ref[...] = weight_ref[...]
    chosen_ref[...] = one_hot(chosen)
    vectors_ref[...] = vector_ref[...]

    def column(values):
        return jnp.sum(jnp.where(chosen, values.astype(F32), 0.0), axis=1, keepdims=True)

    weight, rank, owner = column(weight_ref[...]), column(ids_ref[1:2, :]), column(ids_ref[0:1, :])
    named_ref[...] = one_hot(
        lax.broadcasted_iota(jnp.int32, (nprim, devices), 1).astype(F32) == owner
    ).astype(F32).T.astype(BF16)
    vectors = vector_ref[...] * weight
    for k in range(PAIRS):
        sides = [jnp.where(rank == 2.0 * k + side, vectors, 0.0) for side in range(2)]
        coarse_ref[k * nprim : (k + 1) * nprim, :] = jnp.concatenate(sides, axis=1)
    kb = basis_ref.shape[0]
    fields = [basis_ref[k] for k in range(kb)]
    last_ref[...] = fields[kb - 1]
    total, rest = lane_sums([(fields[i], fields[j]) for i in range(kb) for j in range(i, kb)])
    lane = lax.broadcasted_iota(jnp.int32, (8, LANES), 1)
    gram_ref[...] = jnp.where(lane < 32, pltpu.roll(total, 16, 1), pltpu.roll(rest, 32, 1))
    early.wait()


def restrict_kernel(
    message_ref, ids_ref, weight_ref, chosen_ref, vector_ref, out_ref, contrib_ref
):
    restricted = slots_from_messages(message_ref, ids_ref[0:1, :], ids_ref[1:2, :]) * weight_ref[...]
    out_ref[...] = restricted
    nprim = chosen_ref.shape[0]
    at_prim = sum(mm_nt(chosen_ref[...], part) for part in split(restricted))
    contrib = jnp.sum(at_prim * vector_ref[...], axis=1, keepdims=True)
    square = jnp.broadcast_to(contrib, (nprim, contrib_ref.shape[0])).T
    contrib_ref[...] = jnp.concatenate([square, jnp.zeros((square.shape[0], LANES - nprim), F32)], axis=1)


def neumann_kernel(
    early_ref, blocks_hbm, restricted_ref, ids_ref, weight_ref, message_ref, piece_ref, blocks_ref, sems
):
    width, slots = piece_ref.shape
    held = early_ref.shape[0]
    copies = {}
    for first in range(held // 8 * 8, width, 8):
        start = max(first - held, 0)
        rows = pl.ds(start, first + 8 - held - start)
        copies[first] = pltpu.make_async_copy(
            blocks_hbm.at[pl.ds(start + held, first + 8 - held - start)], blocks_ref.at[rows], sems.at[first // 8]
        )
    for copy in copies.values():
        copy.start()
    for first in range(0, width, 8):
        if first in copies:
            copies[first].wait()
        places = [([early_ref], a) if a < held else ([blocks_ref], a - held) for a in range(first, first + 8)]

        def chunk(c, _, places=places, first=first):
            lanes = pl.ds(pl.multiple_of(c * LANES, LANES), LANES)
            piece_ref[first : first + 8, lanes] = tile_of(places, [restricted_ref[:, lanes]], lanes)
            return 0

        lax.fori_loop(0, slots // LANES, chunk, 0)
    slots_to_messages(piece_ref[...] * weight_ref[...], ids_ref[0:1, :], ids_ref[1:2, :], message_ref)


def correct_kernel(packed_ref, gathered_ref, inverse_ref, coarse_ref, named_ref, message_ref, *, span):
    devices, nprim = named_ref.shape
    ncs = inverse_ref.shape[1]
    contrib = gathered_ref[...][:, :nprim]
    lane = lax.broadcasted_iota(jnp.int32, (nprim, ncs), 1)
    spread = jnp.where(lax.rem(lane, nprim) == lax.broadcasted_iota(jnp.int32, (nprim, ncs), 0), 1.0, 0.0)
    tiled = jnp.dot(contrib, spread, precision=HIGH, preferred_element_type=F32)
    device = lax.broadcasted_iota(jnp.int32, (devices, ncs), 0)
    stream = lax.broadcasted_iota(jnp.int32, (devices, ncs), 1)
    mine = lax.div(device, span) == lax.div(stream, nprim)
    coarse_rhs = jnp.sum(jnp.where(mine, tiled, 0.0), axis=0, keepdims=True)
    coarse_sol = jnp.sum(inverse_ref[...] * coarse_rhs, axis=1, keepdims=True)
    for k in range(PAIRS):
        high, low = split(coarse_ref[k * nprim : (k + 1) * nprim, :] * coarse_sol)
        both = mm(named_ref[...], jnp.concatenate([high, low], axis=1))
        at = message_rows(k, devices)
        message_ref[at, :] = packed_ref[at, :] + (both[:, :LANES] + both[:, LANES:])


def schur_kernel(
    arrived_ref,
    ids_ref,
    index_ref,
    diagonal_ref,
    coupling_ref,
    inverse_ref,
    message_ref,
    gathered_ref,
    inner_ref,
    backward_ref,
):
    kc, inner = index_ref.shape
    chunks = inner // LANES
    owner, rank = ids_ref[0:1, :], ids_ref[1:2, :]
    restored = slots_from_messages(arrived_ref, owner, rank)
    width, slots = restored.shape
    both = jnp.concatenate(split(restored), axis=0)
    for k in range(kc):
        chosen = one_hot(lax.broadcasted_iota(jnp.int32, (slots, inner), 0) == index_ref[k : k + 1, :])
        got = mm(both, chosen)
        gathered_ref[k] = got[:width] + got[width:]
    blocks = [coupling_ref.at[k] for k in range(kc)]
    for c in range(chunks):
        apply_blocks(blocks, [gathered_ref.at[k] for k in range(kc)], inner_ref, c)
        lanes = slice(c * LANES, (c + 1) * LANES)
        vector = inner_ref[:, lanes]

        def step(tile, totals, lanes=lanes, vector=vector):
            for j in range(8):
                a = tile * 8 + j
                solved = block_sums([inverse_ref], [vector], a, lanes)
                totals = tuple(
                    total + ref[a, :, lanes].astype(F32).reshape(width // 8, 8, LANES) * solved[None]
                    for total, ref in zip(totals, blocks)
                )
            return totals

        zero = jnp.zeros((width // 8, 8, LANES), F32)
        totals = lax.fori_loop(0, width // 8, step, (zero,) * kc)
        for k in range(kc):
            backward_ref[k, :, lanes] = totals[k].reshape(width, LANES)
    value = diagonal_ref[...] * restored
    for k in range(kc):
        both = jnp.concatenate(split(backward_ref[k]), axis=0)
        index = as_column(index_ref[k : k + 1, :]).astype(jnp.int32)
        chosen = one_hot(lax.broadcasted_iota(jnp.int32, (inner, slots), 1) == index)
        got = mm(both, chosen)
        value = value - (got[:width] + got[width:])
    slots_to_messages(value, owner, rank, message_ref)


def rows_to_messages(values, asked, message_ref):
    width, rows = values.shape
    devices = asked.shape[1]
    both = jnp.concatenate(split(values), axis=0)
    place = lax.broadcasted_iota(jnp.int32, (rows, devices), 0)
    for k in range(PAIRS):
        chosen = jnp.concatenate(
            [one_hot(place == asked[2 * k : 2 * k + 1]), one_hot(place == asked[2 * k + 1 : 2 * k + 2])], axis=1
        )
        got = mm(both, chosen)
        got = got[:width] + got[width:]
        stacked = jnp.concatenate([got[:, :devices], got[:, devices:]], axis=0)
        message_ref[message_rows(k, devices), :] = stacked.T


def rows_from_messages(message_ref, asked, rows):
    devices = asked.shape[1]
    width = LANES // 2
    place = lax.broadcasted_iota(jnp.int32, (rows, devices), 0)
    totals = [jnp.zeros((rows, 2 * LANES), F32), jnp.zeros((rows, 2 * LANES), F32)]
    for k in range(0, PAIRS, 2):
        parts = []
        for step in (k, k + 1):
            parts.append(jnp.concatenate(split(message_ref[message_rows(step, devices), :]), axis=1))
        parts = jnp.concatenate(parts, axis=0)
        for side in range(2):
            a, b = 2 * k + side, 2 * k + 2 + side
            chosen = jnp.concatenate(
                [one_hot(place == asked[a : a + 1]), one_hot(place == asked[b : b + 1])], axis=1
            )
            totals[side] = totals[side] + mm(chosen, parts)
    sides = [t[:, :LANES] + t[:, LANES:] for t in totals]
    lane = lax.broadcasted_iota(jnp.int32, (rows, LANES), 1)
    both = jnp.where(lane < width, sides[0], sides[1]).T
    return both[:width] + both[width:]


def fetch_kernel(request_ref, vector_ref, asked_ref, message_ref):
    asked = request_ref[...].astype(F32).T.astype(jnp.int32)[: 2 * PAIRS]
    asked_ref[...] = asked
    rows_to_messages(vector_ref[...], asked, message_ref)


def assemble_kernel(arrived_ref, asked_ref, message_ref, *, rows):
    asked = asked_ref[...]
    assembled = rows_from_messages(arrived_ref, asked, rows)
    rows_to_messages(assembled, asked, message_ref)


def two_sum(a, b):
    total = a + b
    back = total - a
    return total, (a - (total - back)) + (b - back)


def pair_add(a, b):
    total, rest = two_sum(a[0], b[0])
    return total, rest + (a[1] + b[1])


def two_product(a, b):
    a_high = a * 4097.0
    a_high = a_high - (a_high - a)
    b_high = b * 4097.0
    b_high = b_high - (b_high - b)
    a_low, b_low = a - a_high, b - b_high
    product = a * b
    return product, ((a_high * b_high - product) + a_high * b_low + a_low * b_high) + a_low * b_low


def lane_sums(products):
    row = lax.broadcasted_iota(jnp.int32, (8, LANES), 0)
    tiles = []
    for base in range(0, len(products), 8):
        tile = (jnp.zeros((8, LANES), F32), jnp.zeros((8, LANES), F32))
        for n, (left, right) in enumerate(products[base : base + 8]):
            width, rows = left.shape
            pair = (jnp.zeros((8, LANES), F32), jnp.zeros((8, LANES), F32))
            for a in range(0, width, 8):
                for b in range(0, rows, LANES):
                    term = left[a : a + 8, b : b + LANES] * right[a : a + 8, b : b + LANES]
                    total, rest = two_sum(pair[0], term)
                    pair = (total, pair[1] + rest)
            for shift in (4, 2, 1):
                pair = pair_add(pair, tuple(pltpu.roll(p, shift, 0) for p in pair))
            tile = tuple(jnp.where(row == n, p, t) for p, t in zip(pair, tile))
        tiles.append(tile)
    pad = [jnp.zeros((LANES - 8 * len(tiles), LANES), F32)]
    pair = tuple(jnp.concatenate([tile[part] for tile in tiles] + pad, axis=0).T for part in range(2))
    half = LANES // 2
    while half >= 8:
        pair = pair_add(tuple(p[:half] for p in pair), tuple(p[half:] for p in pair))
        half //= 2
    for shift in (4, 2, 1):
        pair = pair_add(pair, tuple(pltpu.roll(p, shift, 0) for p in pair))
    return pair


def final_kernel(arrived_ref, asked_ref, basis_ref, gram_ref, image_ref, stats_ref):
    kb, width, rows = basis_ref.shape
    image = rows_from_messages(arrived_ref, asked_ref[...], rows)
    image_ref[...] = image
    total, rest = lane_sums([(image, image)] + [(image, basis_ref[k]) for k in range(kb)])
    lane = lax.broadcasted_iota(jnp.int32, (8, LANES), 1)
    row = jnp.where(lane < 8, total, pltpu.roll(rest, 8, 1))
    row = jnp.where(lane < 16, row, gram_ref[...])
    stats_ref[...] = jnp.concatenate([row] * (stats_ref.shape[0] // 8), axis=0)


def finish_kernel(gathered_ref, image_ref, basis_ref, direction_ref, coeff_ref, *, entries):
    kb = basis_ref.shape[0]
    devices = gathered_ref.shape[0]
    gram = 16
    high = gathered_ref[...]
    lane = lax.broadcasted_iota(jnp.int32, high.shape, 1)
    low = jnp.where(lane < gram, pltpu.roll(high, LANES - 8, 1), pltpu.roll(high, LANES - gram, 1))
    pair = (high, low)
    half = devices // 2
    pair = (high, low)
    while half >= 1:
        pair = pair_add(
            tuple(p[:half] for p in pair), tuple(p[half : 2 * half] for p in pair)
        )
        half //= 2
    lane = lax.broadcasted_iota(jnp.int32, (1, LANES), 1)
    inv_root = 1.0 / math.sqrt(entries)
    projected = (pair[0] + pair[1]) * inv_root
    steps = [
        jnp.sum(jnp.where(lane == 1 + k, projected, 0.0), axis=1, keepdims=True) * inv_root for k in range(kb)
    ]
    left = jnp.where(lane == 0, 1.0, 0.0)
    right = jnp.ones((1, LANES), F32)
    at = gram
    for k in range(kb):
        left = jnp.where(lane == 1 + k, -2.0 * steps[k], left)
        for other in range(k, kb):
            left = jnp.where(lane == at, steps[k] if other == k else 2.0 * steps[k], left)
            right = jnp.where(lane == at, steps[other], right)
            at += 1
    factor, factor_rest = two_product(left, right)
    total, rest = two_product(factor, pair[0])
    pair = (total, rest + (factor * pair[1] + factor_rest * pair[0]))
    shift = gram
    while shift:
        pair = pair_add(pair, tuple(pltpu.roll(p, LANES - shift, 1) for p in pair))
        shift //= 2
    squares = jnp.maximum((pair[0] + pair[1])[:, :1], 0.0)
    root_mean = jnp.sqrt(squares / entries + 1e-06)
    remainder = image_ref[...]
    for k in range(kb):
        remainder = remainder - steps[k] * basis_ref[k]
    direction_ref[...] = remainder * (1.0 / root_mean)
    values = jnp.where(lane == kb, root_mean, pltpu.roll(projected, LANES - 1, 1))
    coeff_ref[...] = values[0, : kb + 1]


def body(
    basis,
    interface_row_owner,
    interface_local_row,
    interface_slot_weight,
    local_inverse,
    prim_index,
    prim_vector,
    coarse_inverse,
    interface_shifted_diagonal,
    coupling_index,
    coupling_blocks,
    interior_inverse,
):
    span = lax.axis_size("span")
    devices = lax.axis_size("stream") * span
    kb, width, rows = basis.shape
    slots = interface_local_row.shape[0]
    kc, inner = coupling_index.shape
    nprim = prim_index.shape[0]
    entries = width * rows * devices
    owner = interface_row_owner.reshape(1, slots)
    row = interface_local_row.reshape(1, slots)
    weight = interface_slot_weight.reshape(1, slots)
    prim = prim_index.reshape(1, nprim)
    shape = jax.ShapeDtypeStruct
    message = shape((devices * PAIRS, LANES), F32)
    field = shape((width, slots), F32)
    square = shape((devices, LANES), F32)

    def exchange(x, per):
        sent = x.reshape(devices, per, LANES)
        return lax.all_to_all(sent, ("stream", "span"), split_axis=0, concat_axis=0, tiled=True).reshape(x.shape)

    anywhere, here = pl.BlockSpec(memory_space=pl.ANY), pl.BlockSpec(memory_space=pltpu.VMEM)
    requests, ids = call(
        plan_kernel,
        (shape((devices, LANES), jnp.int32), shape((2, slots), jnp.int32)),
        owner,
        row,
        vmem=54,
        flops=20_000_000_000,
        in_specs=[anywhere] * 2,
        scratch_shapes=[
            pltpu.VMEM((1, slots), jnp.int32),
            pltpu.VMEM((1, slots), jnp.int32),
            pltpu.SemaphoreType.DMA((2,)),
        ],
    )
    held = 14
    ids, weight, chosen, vectors, coarse, named, gram, last, early = call(
        prepare_kernel,
        (
            shape((2, slots), jnp.int32),
            shape((1, slots), F32),
            shape((nprim, slots), BF16),
            shape((nprim, width), F32),
            shape((PAIRS * nprim, LANES), F32),
            shape((devices, nprim), BF16),
            shape((8, LANES), F32),
            shape((width, rows), F32),
            shape((held, width, slots), BF16),
        ),
        ids,
        weight,
        prim,
        prim_vector.T,
        basis,
        local_inverse,
        vmem=47,
        in_specs=[here] * 5 + [anywhere],
        scratch_shapes=[pltpu.SemaphoreType.DMA],
    )
    arrived = exchange(requests, 1)
    asked, sent = call(fetch_kernel, (shape((2 * PAIRS, devices), jnp.int32), message), arrived, last)
    restricted, contrib = call(
        restrict_kernel, (field, square), exchange(sent, PAIRS), ids, weight, chosen, vectors
    )
    contribs = exchange(contrib, 1)
    packed = call(
        neumann_kernel,
        message,
        early,
        local_inverse,
        restricted,
        ids,
        weight,
        vmem=50,
        in_specs=[here, anywhere, here, here, here],
        scratch_shapes=[
            pltpu.VMEM((width, slots), F32),
            pltpu.VMEM((width - held, width, slots), BF16),
            pltpu.SemaphoreType.DMA((width // 8,)),
        ],
    )
    sent = call(
        functools.partial(correct_kernel, span=span), message, packed, contribs, coarse_inverse, coarse, named
    )
    sent = call(
        functools.partial(assemble_kernel, rows=rows),
        message,
        exchange(sent, PAIRS),
        asked,
        flops=20_000_000_000,
    )
    sent = call(
        schur_kernel,
        message,
        exchange(sent, PAIRS),
        ids,
        coupling_index,
        interface_shifted_diagonal,
        coupling_blocks,
        interior_inverse,
        scratch_shapes=[
            pltpu.VMEM((kc, width, inner), F32),
            pltpu.VMEM((width, inner), F32),
            pltpu.VMEM((kc, width, inner), F32),
        ],
    )
    image, stats = call(
        final_kernel,
        (shape((width, rows), F32), square),
        exchange(sent, PAIRS),
        asked,
        basis,
        gram,
    )
    return call(
        functools.partial(finish_kernel, entries=entries),
        (shape((width, rows), F32), shape((kb + 1,), F32)),
        exchange(stats, 1),
        image,
        basis,
    )


def solution(mesh):
    placed = (
        P(None, None, ("stream", "span")),
        P(("stream", "span"), None),
        P(("stream", "span")),
        P(("stream", "span")),
        P(None, None, ("stream", "span")),
        P(("stream", "span")),
        P(None, ("stream", "span")),
        P("stream", None),
        P(None, ("stream", "span")),
        P(None, ("stream", "span")),
        P(None, None, None, ("stream", "span")),
        P(None, None, ("stream", "span")),
    )
    return jax.shard_map(
        body,
        mesh=mesh,
        in_specs=placed,
        out_specs=(P(None, ("stream", "span")), P()),
        check_vma=False,
    )
```

```python
import functools
import math

import jax
import jax.numpy as jnp
from jax import lax
from jax.experimental import pallas as pl
from jax.experimental.pallas import tpu as pltpu
from jax.sharding import PartitionSpec as P

HIGH = lax.Precision.HIGHEST
F32 = jnp.float32
BF16 = jnp.bfloat16
LANES = 128
PAIRS = 8


def split(x):
    high = x.astype(BF16)
    return high, (x - high.astype(F32)).astype(BF16)


def mm(a, b):
    return jnp.dot(a, b, preferred_element_type=F32)


def mm_nt(a, b, precision=None):
    return lax.dot_general(a, b, (((1,), (1,)), ((), ())), precision=precision, preferred_element_type=F32)


def one_hot(mask):
    return jnp.where(mask, 1.0, 0.0).astype(BF16)


def message_rows(k, count):
    return pl.ds(k, count, stride=PAIRS)


def call(kernel, out_shape, *args, vmem=16, flops=0, **kw):
    if flops:
        kw["cost_estimate"] = pl.CostEstimate(flops=flops, bytes_accessed=flops // 100, transcendentals=0)
    return pl.pallas_call(
        kernel,
        out_shape=out_shape,
        compiler_params=pltpu.CompilerParams(vmem_limit_bytes=vmem * 1024 * 1024),
        **kw,
    )(*args)


def plan_kernel(owner_hbm, row_hbm, request_ref, ids_ref, owner_ref, row_ref, sems):
    slots = owner_ref.shape[1]
    devices = request_ref.shape[0]
    copies = [
        pltpu.make_async_copy(owner_hbm, owner_ref, sems.at[0]),
        pltpu.make_async_copy(row_hbm, row_ref, sems.at[1]),
    ]
    for copy in copies:
        copy.start()
    for copy in copies:
        copy.wait()
    owner = owner_ref[...]
    row = row_ref[...]
    named = one_hot(lax.broadcasted_iota(jnp.int32, (devices, slots), 0) == owner)
    before = lax.broadcasted_iota(jnp.int32, (LANES, LANES), 0) < lax.broadcasted_iota(
        jnp.int32, (LANES, LANES), 1
    )
    counter = jnp.concatenate([one_hot(before), jnp.ones((LANES, LANES), BF16)], axis=1)
    carry = jnp.zeros((devices, LANES), F32)
    ranks = []
    for block in range(slots // LANES):
        part = named[:, block * LANES : (block + 1) * LANES]
        counts = mm(part, counter)
        ranks.append(jnp.sum((counts[:, :LANES] + carry) * part.astype(F32), axis=0, keepdims=True))
        carry = carry + counts[:, LANES:]
    rank = jnp.concatenate(ranks, axis=1).astype(jnp.int32)
    ids_ref[0:1, :] = owner
    ids_ref[1:2, :] = rank
    at_rank = lax.broadcasted_iota(jnp.int32, (LANES, slots), 0) == rank
    tens = jnp.where(at_rank, (row >> 4).astype(F32), 0.0).astype(BF16)
    units = jnp.where(at_rank, (row & 15).astype(F32), 0.0).astype(BF16)
    request_ref[...] = (16.0 * mm_nt(named, tens) + mm_nt(named, units)).astype(jnp.int32)


def slots_from_messages(message_ref, owner, rank):
    slots = owner.shape[1]
    devices = message_ref.shape[0] // PAIRS
    width = LANES // 2
    sides = []
    for k in range(PAIRS):
        high, low = split(message_ref[message_rows(k, devices), :].T)
        sides.append(jnp.concatenate([high, low], axis=1))
    chunk = 256
    pieces = []
    for c in range(slots // chunk):
        lanes = slice(c * chunk, (c + 1) * chunk)
        named = one_hot(lax.broadcasted_iota(jnp.int32, (devices, chunk), 0) == owner[:, lanes])
        named = jnp.concatenate([named, named], axis=0)
        place = jnp.broadcast_to(rank[:, lanes], (8, chunk))
        total = jnp.zeros((width // 8, 8, chunk), F32)
        for k in range(PAIRS):
            both = mm(sides[k], named).reshape(width // 4, 8, chunk)
            total = jnp.where((place == 2 * k)[None], both[: width // 8], total)
            total = jnp.where((place == 2 * k + 1)[None], both[width // 8 :], total)
        pieces.append(total.reshape(width, chunk))
    return jnp.concatenate(pieces, axis=1)


def slots_to_messages(values, owner, rank, message_ref):
    slots = owner.shape[1]
    devices = message_ref.shape[0] // PAIRS
    first = (rank & 1) == 0
    sides = jnp.concatenate([jnp.where(first, values, 0.0), jnp.where(first, 0.0, values)], axis=0).T
    sides = jnp.concatenate(split(sides), axis=1)
    named = one_hot(lax.broadcasted_iota(jnp.int32, (devices, slots), 0) == owner)
    pair = rank >> 1
    for k in range(PAIRS):
        both = mm(named * one_hot(pair == k), sides)
        message_ref[message_rows(k, devices), :] = both[:, :LANES] + both[:, LANES:]


def block_sums(block_refs, vectors, a, lanes):
    total = None
    for ref, vector in zip(block_refs, vectors):
        product = ref[a, :, lanes].astype(F32) * vector
        part = jnp.sum(product.reshape(product.shape[0] // 8, 8, LANES), axis=0)
        total = part if total is None else total + part
    for shift in (4, 2, 1):
        total = total + pltpu.roll(total, shift, 0)
    return total


def row_tile(block_refs, vectors, first, lanes):
    return tile_of([(block_refs, first + j) for j in range(8)], vectors, lanes)


def tile_of(places, vectors, lanes):
    row = lax.broadcasted_iota(jnp.int32, (8, LANES), 0)
    result = jnp.zeros((8, LANES), F32)
    for j, (refs, a) in enumerate(places):
        result = jnp.where(row == j, block_sums(refs, vectors, a, lanes), result)
    return result


def apply_blocks(block_refs, vector_refs, out_ref, c):
    lanes = slice(c * LANES, (c + 1) * LANES)
    vectors = [ref[:, lanes] for ref in vector_refs]

    def rows_of(tile, _):
        first = pl.multiple_of(tile * 8, 8)
        out_ref[pl.ds(first, 8), lanes] = row_tile(block_refs, vectors, first, lanes)
        return 0

    lax.fori_loop(0, out_ref.shape[0] // 8, rows_of, 0)


def as_column(row):
    return jnp.broadcast_to(row.astype(F32), (8, row.shape[1])).T[:, :1]


def prepare_kernel(
    ids_ref,
    weight_ref,
    prim_ref,
    vector_ref,
    basis_ref,
    blocks_hbm,
    kept_ref,
    weights_ref,
    chosen_ref,
    vectors_ref,
    coarse_ref,
    named_ref,
    gram_ref,
    last_ref,
    early_ref,
    sem,
):
    early = pltpu.make_async_copy(blocks_hbm.at[: early_ref.shape[0]], early_ref, sem)
    early.start()
    slots = ids_ref.shape[1]
    nprim = vector_ref.shape[0]
    devices = named_ref.shape[0]
    prim = as_column(prim_ref[...])[:nprim].astype(jnp.int32)
    chosen = lax.broadcasted_iota(jnp.int32, (nprim, slots), 1) == prim
    kept_ref[...] = ids_ref[...]
    weights_ref[...] = weight_ref[...]
    chosen_ref[...] = one_hot(chosen)
    vectors_ref[...] = vector_ref[...]

    def column(values):
        return jnp.sum(jnp.where(chosen, values.astype(F32), 0.0), axis=1, keepdims=True)

    weight, rank, owner = column(weight_ref[...]), column(ids_ref[1:2, :]), column(ids_ref[0:1, :])
    named_ref[...] = one_hot(
        lax.broadcasted_iota(jnp.int32, (nprim, devices), 1).astype(F32) == owner
    ).astype(F32).T.astype(BF16)
    vectors = vector_ref[...] * weight
    for k in range(PAIRS):
        sides = [jnp.where(rank == 2.0 * k + side, vectors, 0.0) for side in range(2)]
        coarse_ref[k * nprim : (k + 1) * nprim, :] = jnp.concatenate(sides, axis=1)
    kb = basis_ref.shape[0]
    fields = [basis_ref[k] for k in range(kb)]
    last_ref[...] = fields[kb - 1]
    total, rest = lane_sums([(fields[i], fields[j]) for i in range(kb) for j in range(i, kb)])
    lane = lax.broadcasted_iota(jnp.int32, (8, LANES), 1)
    gram_ref[...] = jnp.where(lane < 32, pltpu.roll(total, 16, 1), pltpu.roll(rest, 32, 1))
    early.wait()


def restrict_kernel(
    message_ref, ids_ref, weight_ref, chosen_ref, vector_ref, out_ref, contrib_ref
):
    restricted = slots_from_messages(message_ref, ids_ref[0:1, :], ids_ref[1:2, :]) * weight_ref[...]
    out_ref[...] = restricted
    nprim = chosen_ref.shape[0]
    at_prim = sum(mm_nt(chosen_ref[...], part) for part in split(restricted))
    contrib = jnp.sum(at_prim * vector_ref[...], axis=1, keepdims=True)
    square = jnp.broadcast_to(contrib, (nprim, contrib_ref.shape[0])).T
    contrib_ref[...] = jnp.concatenate([square, jnp.zeros((square.shape[0], LANES - nprim), F32)], axis=1)


def neumann_kernel(
    early_ref, blocks_hbm, restricted_ref, ids_ref, weight_ref, message_ref, piece_ref, blocks_ref, sems
):
    width, slots = piece_ref.shape
    held = early_ref.shape[0]
    copies = {}
    for first in range(held // 8 * 8, width, 8):
        start = max(first - held, 0)
        rows = pl.ds(start, first + 8 - held - start)
        copies[first] = pltpu.make_async_copy(
            blocks_hbm.at[pl.ds(start + held, first + 8 - held - start)], blocks_ref.at[rows], sems.at[first // 8]
        )
    for copy in copies.values():
        copy.start()
    for first in range(0, width, 8):
        if first in copies:
            copies[first].wait()
        places = [([early_ref], a) if a < held else ([blocks_ref], a - held) for a in range(first, first + 8)]

        def chunk(c, _, places=places, first=first):
            lanes = pl.ds(pl.multiple_of(c * LANES, LANES), LANES)
            piece_ref[first : first + 8, lanes] = tile_of(places, [restricted_ref[:, lanes]], lanes)
            return 0

        lax.fori_loop(0, slots // LANES, chunk, 0)
    slots_to_messages(piece_ref[...] * weight_ref[...], ids_ref[0:1, :], ids_ref[1:2, :], message_ref)


def correct_kernel(packed_ref, gathered_ref, inverse_ref, coarse_ref, named_ref, message_ref, *, span):
    devices, nprim = named_ref.shape
    ncs = inverse_ref.shape[1]
    streams = devices // span
    group = lax.broadcasted_iota(jnp.int32, (streams, devices), 1)
    group = jnp.where(lax.div(group, span) == lax.broadcasted_iota(jnp.int32, (streams, devices), 0), 1.0, 0.0)
    contrib = jnp.dot(group, gathered_ref[...], precision=HIGH, preferred_element_type=F32)[:, :nprim]
    lane = lax.broadcasted_iota(jnp.int32, (nprim, ncs), 1)
    spread = jnp.where(lax.rem(lane, nprim) == lax.broadcasted_iota(jnp.int32, (nprim, ncs), 0), 1.0, 0.0)
    tiled = jnp.dot(contrib, spread, precision=HIGH, preferred_element_type=F32)
    stream = lax.broadcasted_iota(jnp.int32, (streams, ncs), 0)
    mine = lax.div(lax.broadcasted_iota(jnp.int32, (streams, ncs), 1), nprim) == stream
    coarse_rhs = jnp.sum(jnp.where(mine, tiled, 0.0), axis=0, keepdims=True)
    coarse_sol = jnp.sum(inverse_ref[...] * coarse_rhs, axis=1, keepdims=True)
    for k in range(PAIRS):
        high, low = split(coarse_ref[k * nprim : (k + 1) * nprim, :] * coarse_sol)
        both = mm(named_ref[...], jnp.concatenate([high, low], axis=1))
        at = message_rows(k, devices)
        message_ref[at, :] = packed_ref[at, :] + (both[:, :LANES] + both[:, LANES:])


def schur_kernel(
    arrived_ref,
    ids_ref,
    index_ref,
    diagonal_ref,
    coupling_ref,
    inverse_ref,
    message_ref,
    gathered_ref,
    inner_ref,
    backward_ref,
):
    kc, inner = index_ref.shape
    chunks = inner // LANES
    owner, rank = ids_ref[0:1, :], ids_ref[1:2, :]
    restored = slots_from_messages(arrived_ref, owner, rank)
    width, slots = restored.shape
    both = jnp.concatenate(split(restored), axis=0)
    for k in range(kc):
        chosen = one_hot(lax.broadcasted_iota(jnp.int32, (slots, inner), 0) == index_ref[k : k + 1, :])
        got = mm(both, chosen)
        gathered_ref[k] = got[:width] + got[width:]
    blocks = [coupling_ref.at[k] for k in range(kc)]
    for c in range(chunks):
        apply_blocks(blocks, [gathered_ref.at[k] for k in range(kc)], inner_ref, c)
        lanes = slice(c * LANES, (c + 1) * LANES)
        vector = inner_ref[:, lanes]

        def step(tile, totals, lanes=lanes, vector=vector):
            for j in range(8):
                a = tile * 8 + j
                solved = block_sums([inverse_ref], [vector], a, lanes)
                totals = tuple(
                    total + ref[a, :, lanes].astype(F32).reshape(width // 8, 8, LANES) * solved[None]
                    for total, ref in zip(totals, blocks)
                )
            return totals

        zero = jnp.zeros((width // 8, 8, LANES), F32)
        totals = lax.fori_loop(0, width // 8, step, (zero,) * kc)
        for k in range(kc):
            backward_ref[k, :, lanes] = totals[k].reshape(width, LANES)
    value = diagonal_ref[...] * restored
    for k in range(kc):
        both = jnp.concatenate(split(backward_ref[k]), axis=0)
        index = as_column(index_ref[k : k + 1, :]).astype(jnp.int32)
        chosen = one_hot(lax.broadcasted_iota(jnp.int32, (inner, slots), 1) == index)
        got = mm(both, chosen)
        value = value - (got[:width] + got[width:])
    slots_to_messages(value, owner, rank, message_ref)


def rows_to_messages(values, asked, message_ref):
    width, rows = values.shape
    devices = asked.shape[1]
    both = jnp.concatenate(split(values), axis=0)
    place = lax.broadcasted_iota(jnp.int32, (rows, devices), 0)
    for k in range(PAIRS):
        chosen = jnp.concatenate(
            [one_hot(place == asked[2 * k : 2 * k + 1]), one_hot(place == asked[2 * k + 1 : 2 * k + 2])], axis=1
        )
        got = mm(both, chosen)
        got = got[:width] + got[width:]
        stacked = jnp.concatenate([got[:, :devices], got[:, devices:]], axis=0)
        message_ref[message_rows(k, devices), :] = stacked.T


def rows_from_messages(message_ref, asked, rows):
    devices = asked.shape[1]
    width = LANES // 2
    place = lax.broadcasted_iota(jnp.int32, (rows, devices), 0)
    totals = [jnp.zeros((rows, 2 * LANES), F32), jnp.zeros((rows, 2 * LANES), F32)]
    for k in range(0, PAIRS, 2):
        parts = []
        for step in (k, k + 1):
            parts.append(jnp.concatenate(split(message_ref[message_rows(step, devices), :]), axis=1))
        parts = jnp.concatenate(parts, axis=0)
        for side in range(2):
            a, b = 2 * k + side, 2 * k + 2 + side
            chosen = jnp.concatenate(
                [one_hot(place == asked[a : a + 1]), one_hot(place == asked[b : b + 1])], axis=1
            )
            totals[side] = totals[side] + mm(chosen, parts)
    sides = [t[:, :LANES] + t[:, LANES:] for t in totals]
    lane = lax.broadcasted_iota(jnp.int32, (rows, LANES), 1)
    both = jnp.where(lane < width, sides[0], sides[1]).T
    return both[:width] + both[width:]


def fetch_kernel(request_ref, vector_ref, asked_ref, message_ref):
    asked = request_ref[...].astype(F32).T.astype(jnp.int32)[: 2 * PAIRS]
    asked_ref[...] = asked
    rows_to_messages(vector_ref[...], asked, message_ref)


def assemble_kernel(arrived_ref, asked_ref, message_ref, *, rows):
    asked = asked_ref[...]
    assembled = rows_from_messages(arrived_ref, asked, rows)
    rows_to_messages(assembled, asked, message_ref)


def two_sum(a, b):
    total = a + b
    back = total - a
    return total, (a - (total - back)) + (b - back)


def pair_add(a, b):
    total, rest = two_sum(a[0], b[0])
    return total, rest + (a[1] + b[1])


def two_product(a, b):
    a_high = a * 4097.0
    a_high = a_high - (a_high - a)
    b_high = b * 4097.0
    b_high = b_high - (b_high - b)
    a_low, b_low = a - a_high, b - b_high
    product = a * b
    return product, ((a_high * b_high - product) + a_high * b_low + a_low * b_high) + a_low * b_low


def lane_sums(products):
    row = lax.broadcasted_iota(jnp.int32, (8, LANES), 0)
    tiles = []
    for base in range(0, len(products), 8):
        tile = (jnp.zeros((8, LANES), F32), jnp.zeros((8, LANES), F32))
        for n, (left, right) in enumerate(products[base : base + 8]):
            width, rows = left.shape
            pair = (jnp.zeros((8, LANES), F32), jnp.zeros((8, LANES), F32))
            for a in range(0, width, 8):
                for b in range(0, rows, LANES):
                    term = left[a : a + 8, b : b + LANES] * right[a : a + 8, b : b + LANES]
                    total, rest = two_sum(pair[0], term)
                    pair = (total, pair[1] + rest)
            for shift in (4, 2, 1):
                pair = pair_add(pair, tuple(pltpu.roll(p, shift, 0) for p in pair))
            tile = tuple(jnp.where(row == n, p, t) for p, t in zip(pair, tile))
        tiles.append(tile)
    pad = [jnp.zeros((LANES - 8 * len(tiles), LANES), F32)]
    pair = tuple(jnp.concatenate([tile[part] for tile in tiles] + pad, axis=0).T for part in range(2))
    half = LANES // 2
    while half >= 8:
        pair = pair_add(tuple(p[:half] for p in pair), tuple(p[half:] for p in pair))
        half //= 2
    for shift in (4, 2, 1):
        pair = pair_add(pair, tuple(pltpu.roll(p, shift, 0) for p in pair))
    return pair


def final_kernel(arrived_ref, asked_ref, basis_ref, gram_ref, image_ref, stats_ref):
    kb, width, rows = basis_ref.shape
    image = rows_from_messages(arrived_ref, asked_ref[...], rows)
    image_ref[...] = image
    total, rest = lane_sums([(image, image)] + [(image, basis_ref[k]) for k in range(kb)])
    lane = lax.broadcasted_iota(jnp.int32, (8, LANES), 1)
    row = jnp.where(lane < 8, total, pltpu.roll(rest, 8, 1))
    row = jnp.where(lane < 16, row, gram_ref[...])
    stats_ref[...] = jnp.concatenate([row] * (stats_ref.shape[0] // 8), axis=0)


def finish_kernel(gathered_ref, image_ref, basis_ref, direction_ref, coeff_ref, *, entries):
    kb = basis_ref.shape[0]
    devices = gathered_ref.shape[0]
    gram = 16
    high = gathered_ref[...]
    lane = lax.broadcasted_iota(jnp.int32, high.shape, 1)
    low = jnp.where(lane < gram, pltpu.roll(high, LANES - 8, 1), pltpu.roll(high, LANES - gram, 1))
    pair = (high, low)
    half = devices // 2
    pair = (high, low)
    while half >= 1:
        pair = pair_add(
            tuple(p[:half] for p in pair), tuple(p[half : 2 * half] for p in pair)
        )
        half //= 2
    lane = lax.broadcasted_iota(jnp.int32, (1, LANES), 1)
    inv_root = 1.0 / math.sqrt(entries)
    projected = (pair[0] + pair[1]) * inv_root
    steps = [
        jnp.sum(jnp.where(lane == 1 + k, projected, 0.0), axis=1, keepdims=True) * inv_root for k in range(kb)
    ]
    left = jnp.where(lane == 0, 1.0, 0.0)
    right = jnp.ones((1, LANES), F32)
    at = gram
    for k in range(kb):
        left = jnp.where(lane == 1 + k, -2.0 * steps[k], left)
        for other in range(k, kb):
            left = jnp.where(lane == at, steps[k] if other == k else 2.0 * steps[k], left)
            right = jnp.where(lane == at, steps[other], right)
            at += 1
    factor, factor_rest = two_product(left, right)
    total, rest = two_product(factor, pair[0])
    pair = (total, rest + (factor * pair[1] + factor_rest * pair[0]))
    shift = gram
    while shift:
        pair = pair_add(pair, tuple(pltpu.roll(p, LANES - shift, 1) for p in pair))
        shift //= 2
    squares = jnp.maximum((pair[0] + pair[1])[:, :1], 0.0)
    root_mean = jnp.sqrt(squares / entries + 1e-06)
    remainder = image_ref[...]
    for k in range(kb):
        remainder = remainder - steps[k] * basis_ref[k]
    direction_ref[...] = remainder * (1.0 / root_mean)
    values = jnp.where(lane == kb, root_mean, pltpu.roll(projected, LANES - 1, 1))
    coeff_ref[...] = values[0, : kb + 1]


def body(
    basis,
    interface_row_owner,
    interface_local_row,
    interface_slot_weight,
    local_inverse,
    prim_index,
    prim_vector,
    coarse_inverse,
    interface_shifted_diagonal,
    coupling_index,
    coupling_blocks,
    interior_inverse,
):
    span = lax.axis_size("span")
    devices = lax.axis_size("stream") * span
    kb, width, rows = basis.shape
    slots = interface_local_row.shape[0]
    kc, inner = coupling_index.shape
    nprim = prim_index.shape[0]
    entries = width * rows * devices
    owner = interface_row_owner.reshape(1, slots)
    row = interface_local_row.reshape(1, slots)
    weight = interface_slot_weight.reshape(1, slots)
    prim = prim_index.reshape(1, nprim)
    shape = jax.ShapeDtypeStruct
    message = shape((devices * PAIRS, LANES), F32)
    field = shape((width, slots), F32)
    square = shape((devices, LANES), F32)

    def exchange(x, per):
        sent = x.reshape(devices, per, LANES)
        return lax.all_to_all(sent, ("stream", "span"), split_axis=0, concat_axis=0, tiled=True).reshape(x.shape)

    anywhere, here = pl.BlockSpec(memory_space=pl.ANY), pl.BlockSpec(memory_space=pltpu.VMEM)
    requests, ids = call(
        plan_kernel,
        (shape((devices, LANES), jnp.int32), shape((2, slots), jnp.int32)),
        owner,
        row,
        vmem=54,
        flops=20_000_000_000,
        in_specs=[anywhere] * 2,
        scratch_shapes=[
            pltpu.VMEM((1, slots), jnp.int32),
            pltpu.VMEM((1, slots), jnp.int32),
            pltpu.SemaphoreType.DMA((2,)),
        ],
    )
    held = 14
    ids, weight, chosen, vectors, coarse, named, gram, last, early = call(
        prepare_kernel,
        (
            shape((2, slots), jnp.int32),
            shape((1, slots), F32),
            shape((nprim, slots), BF16),
            shape((nprim, width), F32),
            shape((PAIRS * nprim, LANES), F32),
            shape((devices, nprim), BF16),
            shape((8, LANES), F32),
            shape((width, rows), F32),
            shape((held, width, slots), BF16),
        ),
        ids,
        weight,
        prim,
        prim_vector.T,
        basis,
        local_inverse,
        vmem=47,
        in_specs=[here] * 5 + [anywhere],
        scratch_shapes=[pltpu.SemaphoreType.DMA],
    )
    arrived = exchange(requests, 1)
    asked, sent = call(fetch_kernel, (shape((2 * PAIRS, devices), jnp.int32), message), arrived, last)
    restricted, contrib = call(
        restrict_kernel, (field, square), exchange(sent, PAIRS), ids, weight, chosen, vectors
    )
    contribs = exchange(contrib, 1)
    packed = call(
        neumann_kernel,
        message,
        early,
        local_inverse,
        restricted,
        ids,
        weight,
        vmem=50,
        in_specs=[here, anywhere, here, here, here],
        scratch_shapes=[
            pltpu.VMEM((width, slots), F32),
            pltpu.VMEM((width - held, width, slots), BF16),
            pltpu.SemaphoreType.DMA((width // 8,)),
        ],
    )
    sent = call(
        functools.partial(correct_kernel, span=span), message, packed, contribs, coarse_inverse, coarse, named
    )
    sent = call(
        functools.partial(assemble_kernel, rows=rows),
        message,
        exchange(sent, PAIRS),
        asked,
        flops=20_000_000_000,
    )
    sent = call(
        schur_kernel,
        message,
        exchange(sent, PAIRS),
        ids,
        coupling_index,
        interface_shifted_diagonal,
        coupling_blocks,
        interior_inverse,
        scratch_shapes=[
            pltpu.VMEM((kc, width, inner), F32),
            pltpu.VMEM((width, inner), F32),
            pltpu.VMEM((kc, width, inner), F32),
        ],
    )
    image, stats = call(
        final_kernel,
        (shape((width, rows), F32), square),
        exchange(sent, PAIRS),
        asked,
        basis,
        gram,
    )
    return call(
        functools.partial(finish_kernel, entries=entries),
        (shape((width, rows), F32), shape((kb + 1,), F32)),
        exchange(stats, 1),
        image,
        basis,
    )


def solution(mesh):
    placed = (
        P(None, None, ("stream", "span")),
        P(("stream", "span"), None),
        P(("stream", "span")),
        P(("stream", "span")),
        P(None, None, ("stream", "span")),
        P(("stream", "span")),
        P(None, ("stream", "span")),
        P("stream", None),
        P(None, ("stream", "span")),
        P(None, ("stream", "span")),
        P(None, None, None, ("stream", "span")),
        P(None, None, ("stream", "span")),
    )
    return jax.shard_map(
        body,
        mesh=mesh,
        in_specs=placed,
        out_specs=(P(None, ("stream", "span")), P()),
        check_vma=False,
    )
```

```python
import functools
import math

import jax
import jax.numpy as jnp
from jax import lax
from jax.experimental import pallas as pl
from jax.experimental.pallas import tpu as pltpu
from jax.sharding import PartitionSpec as P

HIGH = lax.Precision.HIGHEST
F32 = jnp.float32
BF16 = jnp.bfloat16
LANES = 128
PAIRS = 8


def split(x):
    high = x.astype(BF16)
    return high, (x - high.astype(F32)).astype(BF16)


def mm(a, b):
    return jnp.dot(a, b, preferred_element_type=F32)


def mm_nt(a, b, precision=None):
    return lax.dot_general(a, b, (((1,), (1,)), ((), ())), precision=precision, preferred_element_type=F32)


def one_hot(mask):
    return jnp.where(mask, 1.0, 0.0).astype(BF16)


def message_rows(k, count):
    return pl.ds(k, count, stride=PAIRS)


def call(kernel, out_shape, *args, vmem=16, flops=0, **kw):
    if flops:
        kw["cost_estimate"] = pl.CostEstimate(flops=flops, bytes_accessed=flops // 100, transcendentals=0)
    return pl.pallas_call(
        kernel,
        out_shape=out_shape,
        compiler_params=pltpu.CompilerParams(vmem_limit_bytes=vmem * 1024 * 1024),
        **kw,
    )(*args)


def plan_kernel(owner_hbm, row_hbm, request_ref, ids_ref, owner_ref, row_ref, sems):
    slots = owner_ref.shape[1]
    devices = request_ref.shape[0]
    copies = [
        pltpu.make_async_copy(owner_hbm, owner_ref, sems.at[0]),
        pltpu.make_async_copy(row_hbm, row_ref, sems.at[1]),
    ]
    for copy in copies:
        copy.start()
    for copy in copies:
        copy.wait()
    owner = owner_ref[...]
    row = row_ref[...]
    named = one_hot(lax.broadcasted_iota(jnp.int32, (devices, slots), 0) == owner)
    before = lax.broadcasted_iota(jnp.int32, (LANES, LANES), 0) < lax.broadcasted_iota(
        jnp.int32, (LANES, LANES), 1
    )
    counter = jnp.concatenate([one_hot(before), jnp.ones((LANES, LANES), BF16)], axis=1)
    carry = jnp.zeros((devices, LANES), F32)
    ranks = []
    for block in range(slots // LANES):
        part = named[:, block * LANES : (block + 1) * LANES]
        counts = mm(part, counter)
        ranks.append(jnp.sum((counts[:, :LANES] + carry) * part.astype(F32), axis=0, keepdims=True))
        carry = carry + counts[:, LANES:]
    rank = jnp.concatenate(ranks, axis=1).astype(jnp.int32)
    ids_ref[0:1, :] = owner
    ids_ref[1:2, :] = rank
    at_rank = lax.broadcasted_iota(jnp.int32, (LANES, slots), 0) == rank
    tens = jnp.where(at_rank, (row >> 4).astype(F32), 0.0).astype(BF16)
    units = jnp.where(at_rank, (row & 15).astype(F32), 0.0).astype(BF16)
    request_ref[...] = (16.0 * mm_nt(named, tens) + mm_nt(named, units)).astype(jnp.int32)


def slots_from_messages(message_ref, owner, rank):
    slots = owner.shape[1]
    devices = message_ref.shape[0] // PAIRS
    width = LANES // 2
    sides = []
    for k in range(PAIRS):
        high, low = split(message_ref[message_rows(k, devices), :].T)
        sides.append(jnp.concatenate([high, low], axis=1))
    chunk = 256
    pieces = []
    for c in range(slots // chunk):
        lanes = slice(c * chunk, (c + 1) * chunk)
        named = one_hot(lax.broadcasted_iota(jnp.int32, (devices, chunk), 0) == owner[:, lanes])
        named = jnp.concatenate([named, named], axis=0)
        place = jnp.broadcast_to(rank[:, lanes], (8, chunk))
        total = jnp.zeros((width // 8, 8, chunk), F32)
        for k in range(PAIRS):
            both = mm(sides[k], named).reshape(width // 4, 8, chunk)
            total = jnp.where((place == 2 * k)[None], both[: width // 8], total)
            total = jnp.where((place == 2 * k + 1)[None], both[width // 8 :], total)
        pieces.append(total.reshape(width, chunk))
    return jnp.concatenate(pieces, axis=1)


def slots_to_messages(values, owner, rank, message_ref):
    slots = owner.shape[1]
    devices = message_ref.shape[0] // PAIRS
    first = (rank & 1) == 0
    sides = jnp.concatenate([jnp.where(first, values, 0.0), jnp.where(first, 0.0, values)], axis=0).T
    sides = jnp.concatenate(split(sides), axis=1)
    named = one_hot(lax.broadcasted_iota(jnp.int32, (devices, slots), 0) == owner)
    pair = rank >> 1
    for k in range(PAIRS):
        both = mm(named * one_hot(pair == k), sides)
        message_ref[message_rows(k, devices), :] = both[:, :LANES] + both[:, LANES:]


def block_sums(block_refs, vectors, a, lanes):
    total = None
    for ref, vector in zip(block_refs, vectors):
        product = ref[a, :, lanes].astype(F32) * vector
        part = jnp.sum(product.reshape(product.shape[0] // 8, 8, LANES), axis=0)
        total = part if total is None else total + part
    for shift in (4, 2, 1):
        total = total + pltpu.roll(total, shift, 0)
    return total


def row_tile(block_refs, vectors, first, lanes):
    return tile_of([(block_refs, first + j) for j in range(8)], vectors, lanes)


def tile_of(places, vectors, lanes):
    row = lax.broadcasted_iota(jnp.int32, (8, LANES), 0)
    result = jnp.zeros((8, LANES), F32)
    for j, (refs, a) in enumerate(places):
        result = jnp.where(row == j, block_sums(refs, vectors, a, lanes), result)
    return result


def apply_blocks(block_refs, vector_refs, out_ref, c):
    lanes = slice(c * LANES, (c + 1) * LANES)
    vectors = [ref[:, lanes] for ref in vector_refs]

    def rows_of(tile, _):
        first = pl.multiple_of(tile * 8, 8)
        out_ref[pl.ds(first, 8), lanes] = row_tile(block_refs, vectors, first, lanes)
        return 0

    lax.fori_loop(0, out_ref.shape[0] // 8, rows_of, 0)


def as_column(row):
    return jnp.broadcast_to(row.astype(F32), (8, row.shape[1])).T[:, :1]


def prepare_kernel(
    ids_ref,
    weight_ref,
    prim_ref,
    vector_ref,
    basis_ref,
    blocks_hbm,
    kept_ref,
    weights_ref,
    chosen_ref,
    vectors_ref,
    coarse_ref,
    named_ref,
    gram_ref,
    last_ref,
    early_ref,
    sem,
):
    early = pltpu.make_async_copy(blocks_hbm.at[: early_ref.shape[0]], early_ref, sem)
    early.start()
    slots = ids_ref.shape[1]
    nprim = vector_ref.shape[0]
    devices = named_ref.shape[0]
    prim = as_column(prim_ref[...])[:nprim].astype(jnp.int32)
    chosen = lax.broadcasted_iota(jnp.int32, (nprim, slots), 1) == prim
    kept_ref[...] = ids_ref[...]
    weights_ref[...] = weight_ref[...]
    chosen_ref[...] = one_hot(chosen)
    vectors_ref[...] = vector_ref[...]

    def column(values):
        return jnp.sum(jnp.where(chosen, values.astype(F32), 0.0), axis=1, keepdims=True)

    weight, rank, owner = column(weight_ref[...]), column(ids_ref[1:2, :]), column(ids_ref[0:1, :])
    named_ref[...] = one_hot(
        lax.broadcasted_iota(jnp.int32, (nprim, devices), 1).astype(F32) == owner
    ).astype(F32).T.astype(BF16)
    vectors = vector_ref[...] * weight
    for k in range(PAIRS):
        sides = [jnp.where(rank == 2.0 * k + side, vectors, 0.0) for side in range(2)]
        coarse_ref[k * nprim : (k + 1) * nprim, :] = jnp.concatenate(sides, axis=1)
    kb = basis_ref.shape[0]
    fields = [basis_ref[k] for k in range(kb)]
    last_ref[...] = fields[kb - 1]
    total, rest = lane_sums([(fields[i], fields[j]) for i in range(kb) for j in range(i, kb)])
    lane = lax.broadcasted_iota(jnp.int32, (8, LANES), 1)
    gram_ref[...] = jnp.where(lane < 32, pltpu.roll(total, 16, 1), pltpu.roll(rest, 32, 1))
    early.wait()


def restrict_kernel(
    message_ref, ids_ref, weight_ref, chosen_ref, vector_ref, out_ref, contrib_ref
):
    restricted = slots_from_messages(message_ref, ids_ref[0:1, :], ids_ref[1:2, :]) * weight_ref[...]
    out_ref[...] = restricted
    nprim = chosen_ref.shape[0]
    at_prim = sum(mm_nt(chosen_ref[...], part) for part in split(restricted))
    contrib = jnp.sum(at_prim * vector_ref[...], axis=1, keepdims=True)
    square = jnp.broadcast_to(contrib, (nprim, contrib_ref.shape[0])).T
    contrib_ref[...] = jnp.concatenate([square, jnp.zeros((square.shape[0], LANES - nprim), F32)], axis=1)


def neumann_kernel(
    early_ref, blocks_hbm, restricted_ref, ids_ref, weight_ref, message_ref, piece_ref, blocks_ref, sems
):
    width, slots = piece_ref.shape
    held = early_ref.shape[0]
    copies = {}
    for first in range(held // 8 * 8, width, 8):
        start = max(first - held, 0)
        rows = pl.ds(start, first + 8 - held - start)
        copies[first] = pltpu.make_async_copy(
            blocks_hbm.at[pl.ds(start + held, first + 8 - held - start)], blocks_ref.at[rows], sems.at[first // 8]
        )
    ahead = 24
    for first in range(0, held // 8 * 8 + ahead, 8):
        if first in copies:
            copies[first].start()
    for first in range(0, width, 8):
        if first in copies:
            copies[first].wait()
            if first + ahead in copies:
                copies[first + ahead].start()
        places = [([early_ref], a) if a < held else ([blocks_ref], a - held) for a in range(first, first + 8)]

        def chunk(c, _, places=places, first=first):
            lanes = pl.ds(pl.multiple_of(c * LANES, LANES), LANES)
            piece_ref[first : first + 8, lanes] = tile_of(places, [restricted_ref[:, lanes]], lanes)
            return 0

        lax.fori_loop(0, slots // LANES, chunk, 0)
    slots_to_messages(piece_ref[...] * weight_ref[...], ids_ref[0:1, :], ids_ref[1:2, :], message_ref)


def correct_kernel(packed_ref, gathered_ref, inverse_ref, coarse_ref, named_ref, message_ref, *, span):
    devices, nprim = named_ref.shape
    ncs = inverse_ref.shape[1]
    streams = devices // span
    group = lax.broadcasted_iota(jnp.int32, (streams, devices), 1)
    group = jnp.where(lax.div(group, span) == lax.broadcasted_iota(jnp.int32, (streams, devices), 0), 1.0, 0.0)
    contrib = jnp.dot(group, gathered_ref[...], precision=HIGH, preferred_element_type=F32)[:, :nprim]
    lane = lax.broadcasted_iota(jnp.int32, (nprim, ncs), 1)
    spread = jnp.where(lax.rem(lane, nprim) == lax.broadcasted_iota(jnp.int32, (nprim, ncs), 0), 1.0, 0.0)
    tiled = jnp.dot(contrib, spread, precision=HIGH, preferred_element_type=F32)
    stream = lax.broadcasted_iota(jnp.int32, (streams, ncs), 0)
    mine = lax.div(lax.broadcasted_iota(jnp.int32, (streams, ncs), 1), nprim) == stream
    coarse_rhs = jnp.sum(jnp.where(mine, tiled, 0.0), axis=0, keepdims=True)
    coarse_sol = jnp.sum(inverse_ref[...] * coarse_rhs, axis=1, keepdims=True)
    for k in range(PAIRS):
        high, low = split(coarse_ref[k * nprim : (k + 1) * nprim, :] * coarse_sol)
        both = mm(named_ref[...], jnp.concatenate([high, low], axis=1))
        at = message_rows(k, devices)
        message_ref[at, :] = packed_ref[at, :] + (both[:, :LANES] + both[:, LANES:])


def schur_kernel(
    arrived_ref,
    ids_ref,
    index_ref,
    diagonal_ref,
    coupling_ref,
    inverse_ref,
    message_ref,
    gathered_ref,
    inner_ref,
    backward_ref,
):
    kc, inner = index_ref.shape
    chunks = inner // LANES
    owner, rank = ids_ref[0:1, :], ids_ref[1:2, :]
    restored = slots_from_messages(arrived_ref, owner, rank)
    width, slots = restored.shape
    both = jnp.concatenate(split(restored), axis=0)
    for k in range(kc):
        chosen = one_hot(lax.broadcasted_iota(jnp.int32, (slots, inner), 0) == index_ref[k : k + 1, :])
        got = mm(both, chosen)
        gathered_ref[k] = got[:width] + got[width:]
    blocks = [coupling_ref.at[k] for k in range(kc)]
    for c in range(chunks):
        apply_blocks(blocks, [gathered_ref.at[k] for k in range(kc)], inner_ref, c)
        lanes = slice(c * LANES, (c + 1) * LANES)
        vector = inner_ref[:, lanes]

        def step(tile, totals, lanes=lanes, vector=vector):
            for j in range(8):
                a = tile * 8 + j
                solved = block_sums([inverse_ref], [vector], a, lanes)
                totals = tuple(
                    total + ref[a, :, lanes].astype(F32).reshape(width // 8, 8, LANES) * solved[None]
                    for total, ref in zip(totals, blocks)
                )
            return totals

        zero = jnp.zeros((width // 8, 8, LANES), F32)
        totals = lax.fori_loop(0, width // 8, step, (zero,) * kc)
        for k in range(kc):
            backward_ref[k, :, lanes] = totals[k].reshape(width, LANES)
    value = diagonal_ref[...] * restored
    for k in range(kc):
        both = jnp.concatenate(split(backward_ref[k]), axis=0)
        index = as_column(index_ref[k : k + 1, :]).astype(jnp.int32)
        chosen = one_hot(lax.broadcasted_iota(jnp.int32, (inner, slots), 1) == index)
        got = mm(both, chosen)
        value = value - (got[:width] + got[width:])
    slots_to_messages(value, owner, rank, message_ref)


def rows_to_messages(values, asked, message_ref):
    width, rows = values.shape
    devices = asked.shape[1]
    both = jnp.concatenate(split(values), axis=0)
    place = lax.broadcasted_iota(jnp.int32, (rows, devices), 0)
    for k in range(PAIRS):
        chosen = jnp.concatenate(
            [one_hot(place == asked[2 * k : 2 * k + 1]), one_hot(place == asked[2 * k + 1 : 2 * k + 2])], axis=1
        )
        got = mm(both, chosen)
        got = got[:width] + got[width:]
        stacked = jnp.concatenate([got[:, :devices], got[:, devices:]], axis=0)
        message_ref[message_rows(k, devices), :] = stacked.T


def rows_from_messages(message_ref, asked, rows):
    devices = asked.shape[1]
    width = LANES // 2
    place = lax.broadcasted_iota(jnp.int32, (rows, devices), 0)
    totals = [jnp.zeros((rows, 2 * LANES), F32), jnp.zeros((rows, 2 * LANES), F32)]
    for k in range(0, PAIRS, 2):
        parts = []
        for step in (k, k + 1):
            parts.append(jnp.concatenate(split(message_ref[message_rows(step, devices), :]), axis=1))
        parts = jnp.concatenate(parts, axis=0)
        for side in range(2):
            a, b = 2 * k + side, 2 * k + 2 + side
            chosen = jnp.concatenate(
                [one_hot(place == asked[a : a + 1]), one_hot(place == asked[b : b + 1])], axis=1
            )
            totals[side] = totals[side] + mm(chosen, parts)
    sides = [t[:, :LANES] + t[:, LANES:] for t in totals]
    lane = lax.broadcasted_iota(jnp.int32, (rows, LANES), 1)
    both = jnp.where(lane < width, sides[0], sides[1]).T
    return both[:width] + both[width:]


def fetch_kernel(request_ref, vector_ref, asked_ref, message_ref):
    asked = request_ref[...].astype(F32).T.astype(jnp.int32)[: 2 * PAIRS]
    asked_ref[...] = asked
    rows_to_messages(vector_ref[...], asked, message_ref)


def assemble_kernel(arrived_ref, asked_ref, message_ref, *, rows):
    asked = asked_ref[...]
    assembled = rows_from_messages(arrived_ref, asked, rows)
    rows_to_messages(assembled, asked, message_ref)


def two_sum(a, b):
    total = a + b
    back = total - a
    return total, (a - (total - back)) + (b - back)


def pair_add(a, b):
    total, rest = two_sum(a[0], b[0])
    return total, rest + (a[1] + b[1])


def two_product(a, b):
    a_high = a * 4097.0
    a_high = a_high - (a_high - a)
    b_high = b * 4097.0
    b_high = b_high - (b_high - b)
    a_low, b_low = a - a_high, b - b_high
    product = a * b
    return product, ((a_high * b_high - product) + a_high * b_low + a_low * b_high) + a_low * b_low


def lane_sums(products):
    row = lax.broadcasted_iota(jnp.int32, (8, LANES), 0)
    tiles = []
    for base in range(0, len(products), 8):
        tile = (jnp.zeros((8, LANES), F32), jnp.zeros((8, LANES), F32))
        for n, (left, right) in enumerate(products[base : base + 8]):
            width, rows = left.shape
            pair = (jnp.zeros((8, LANES), F32), jnp.zeros((8, LANES), F32))
            for a in range(0, width, 8):
                for b in range(0, rows, LANES):
                    term = left[a : a + 8, b : b + LANES] * right[a : a + 8, b : b + LANES]
                    total, rest = two_sum(pair[0], term)
                    pair = (total, pair[1] + rest)
            for shift in (4, 2, 1):
                pair = pair_add(pair, tuple(pltpu.roll(p, shift, 0) for p in pair))
            tile = tuple(jnp.where(row == n, p, t) for p, t in zip(pair, tile))
        tiles.append(tile)
    pad = [jnp.zeros((LANES - 8 * len(tiles), LANES), F32)]
    pair = tuple(jnp.concatenate([tile[part] for tile in tiles] + pad, axis=0).T for part in range(2))
    half = LANES // 2
    while half >= 8:
        pair = pair_add(tuple(p[:half] for p in pair), tuple(p[half:] for p in pair))
        half //= 2
    for shift in (4, 2, 1):
        pair = pair_add(pair, tuple(pltpu.roll(p, shift, 0) for p in pair))
    return pair


def final_kernel(arrived_ref, asked_ref, basis_ref, gram_ref, image_ref, stats_ref):
    kb, width, rows = basis_ref.shape
    image = rows_from_messages(arrived_ref, asked_ref[...], rows)
    image_ref[...] = image
    total, rest = lane_sums([(image, image)] + [(image, basis_ref[k]) for k in range(kb)])
    lane = lax.broadcasted_iota(jnp.int32, (8, LANES), 1)
    row = jnp.where(lane < 8, total, pltpu.roll(rest, 8, 1))
    row = jnp.where(lane < 16, row, gram_ref[...])
    stats_ref[...] = jnp.concatenate([row] * (stats_ref.shape[0] // 8), axis=0)


def finish_kernel(gathered_ref, image_ref, basis_ref, direction_ref, coeff_ref, *, entries):
    kb = basis_ref.shape[0]
    devices = gathered_ref.shape[0]
    gram = 16
    high = gathered_ref[...]
    lane = lax.broadcasted_iota(jnp.int32, high.shape, 1)
    low = jnp.where(lane < gram, pltpu.roll(high, LANES - 8, 1), pltpu.roll(high, LANES - gram, 1))
    pair = (high, low)
    half = devices // 2
    pair = (high, low)
    while half >= 1:
        pair = pair_add(
            tuple(p[:half] for p in pair), tuple(p[half : 2 * half] for p in pair)
        )
        half //= 2
    lane = lax.broadcasted_iota(jnp.int32, (1, LANES), 1)
    inv_root = 1.0 / math.sqrt(entries)
    projected = (pair[0] + pair[1]) * inv_root
    steps = [
        jnp.sum(jnp.where(lane == 1 + k, projected, 0.0), axis=1, keepdims=True) * inv_root for k in range(kb)
    ]
    left = jnp.where(lane == 0, 1.0, 0.0)
    right = jnp.ones((1, LANES), F32)
    at = gram
    for k in range(kb):
        left = jnp.where(lane == 1 + k, -2.0 * steps[k], left)
        for other in range(k, kb):
            left = jnp.where(lane == at, steps[k] if other == k else 2.0 * steps[k], left)
            right = jnp.where(lane == at, steps[other], right)
            at += 1
    factor, factor_rest = two_product(left, right)
    total, rest = two_product(factor, pair[0])
    pair = (total, rest + (factor * pair[1] + factor_rest * pair[0]))
    shift = gram
    while shift:
        pair = pair_add(pair, tuple(pltpu.roll(p, LANES - shift, 1) for p in pair))
        shift //= 2
    squares = jnp.maximum((pair[0] + pair[1])[:, :1], 0.0)
    root_mean = jnp.sqrt(squares / entries + 1e-06)
    remainder = image_ref[...]
    for k in range(kb):
        remainder = remainder - steps[k] * basis_ref[k]
    direction_ref[...] = remainder * (1.0 / root_mean)
    values = jnp.where(lane == kb, root_mean, pltpu.roll(projected, LANES - 1, 1))
    coeff_ref[...] = values[0, : kb + 1]


def body(
    basis,
    interface_row_owner,
    interface_local_row,
    interface_slot_weight,
    local_inverse,
    prim_index,
    prim_vector,
    coarse_inverse,
    interface_shifted_diagonal,
    coupling_index,
    coupling_blocks,
    interior_inverse,
):
    span = lax.axis_size("span")
    devices = lax.axis_size("stream") * span
    kb, width, rows = basis.shape
    slots = interface_local_row.shape[0]
    kc, inner = coupling_index.shape
    nprim = prim_index.shape[0]
    entries = width * rows * devices
    owner = interface_row_owner.reshape(1, slots)
    row = interface_local_row.reshape(1, slots)
    weight = interface_slot_weight.reshape(1, slots)
    prim = prim_index.reshape(1, nprim)
    shape = jax.ShapeDtypeStruct
    message = shape((devices * PAIRS, LANES), F32)
    field = shape((width, slots), F32)
    square = shape((devices, LANES), F32)

    def exchange(x, per):
        sent = x.reshape(devices, per, LANES)
        return lax.all_to_all(sent, ("stream", "span"), split_axis=0, concat_axis=0, tiled=True).reshape(x.shape)

    anywhere, here = pl.BlockSpec(memory_space=pl.ANY), pl.BlockSpec(memory_space=pltpu.VMEM)
    requests, ids = call(
        plan_kernel,
        (shape((devices, LANES), jnp.int32), shape((2, slots), jnp.int32)),
        owner,
        row,
        vmem=54,
        flops=20_000_000_000,
        in_specs=[anywhere] * 2,
        scratch_shapes=[
            pltpu.VMEM((1, slots), jnp.int32),
            pltpu.VMEM((1, slots), jnp.int32),
            pltpu.SemaphoreType.DMA((2,)),
        ],
    )
    held = 14
    ids, weight, chosen, vectors, coarse, named, gram, last, early = call(
        prepare_kernel,
        (
            shape((2, slots), jnp.int32),
            shape((1, slots), F32),
            shape((nprim, slots), BF16),
            shape((nprim, width), F32),
            shape((PAIRS * nprim, LANES), F32),
            shape((devices, nprim), BF16),
            shape((8, LANES), F32),
            shape((width, rows), F32),
            shape((held, width, slots), BF16),
        ),
        ids,
        weight,
        prim,
        prim_vector.T,
        basis,
        local_inverse,
        vmem=47,
        in_specs=[here] * 5 + [anywhere],
        scratch_shapes=[pltpu.SemaphoreType.DMA],
    )
    arrived = exchange(requests, 1)
    asked, sent = call(fetch_kernel, (shape((2 * PAIRS, devices), jnp.int32), message), arrived, last)
    restricted, contrib = call(
        restrict_kernel, (field, square), exchange(sent, PAIRS), ids, weight, chosen, vectors
    )
    contribs = exchange(contrib, 1)
    packed = call(
        neumann_kernel,
        message,
        early,
        local_inverse,
        restricted,
        ids,
        weight,
        vmem=50,
        in_specs=[here, anywhere, here, here, here],
        scratch_shapes=[
            pltpu.VMEM((width, slots), F32),
            pltpu.VMEM((width - held, width, slots), BF16),
            pltpu.SemaphoreType.DMA((width // 8,)),
        ],
    )
    sent = call(
        functools.partial(correct_kernel, span=span), message, packed, contribs, coarse_inverse, coarse, named
    )
    sent = call(
        functools.partial(assemble_kernel, rows=rows),
        message,
        exchange(sent, PAIRS),
        asked,
        flops=20_000_000_000,
    )
    sent = call(
        schur_kernel,
        message,
        exchange(sent, PAIRS),
        ids,
        coupling_index,
        interface_shifted_diagonal,
        coupling_blocks,
        interior_inverse,
        scratch_shapes=[
            pltpu.VMEM((kc, width, inner), F32),
            pltpu.VMEM((width, inner), F32),
            pltpu.VMEM((kc, width, inner), F32),
        ],
    )
    image, stats = call(
        final_kernel,
        (shape((width, rows), F32), square),
        exchange(sent, PAIRS),
        asked,
        basis,
        gram,
    )
    return call(
        functools.partial(finish_kernel, entries=entries),
        (shape((width, rows), F32), shape((kb + 1,), F32)),
        exchange(stats, 1),
        image,
        basis,
    )


def solution(mesh):
    placed = (
        P(None, None, ("stream", "span")),
        P(("stream", "span"), None),
        P(("stream", "span")),
        P(("stream", "span")),
        P(None, None, ("stream", "span")),
        P(("stream", "span")),
        P(None, ("stream", "span")),
        P("stream", None),
        P(None, ("stream", "span")),
        P(None, ("stream", "span")),
        P(None, None, None, ("stream", "span")),
        P(None, None, ("stream", "span")),
    )
    return jax.shard_map(
        body,
        mesh=mesh,
        in_specs=placed,
        out_specs=(P(None, ("stream", "span")), P()),
        check_vma=False,
    )
```
